128 devices in a mesh: resp: 16 (over y_lo, z, core), tp: 8 (over x, y_hi).
Axes of the slice: x: 4, y: 4 (y_hi: 2, y_lo: 2; y = y_hi * 2 + y_lo), z: 4, core: 2. Of those that a mesh axis runs over, the one named last changes fastest.
Arguments:
- queries: bfloat16 [8192, 8192], P('resp', 'tp'), may hold values from -8 to 8
- out_grad: bfloat16 [8192, 8192], P('resp', 'tp'), may hold values from -6 to 6
- resp_kv: bfloat16 [8192, 2048], P('resp', 'tp'), may hold values from -6 to 6
- prefix_kv: bfloat16 [2048, 2048], P('resp', 'tp'), may hold values from -8 to 8
- q_weight: bfloat16 [5120, 8192], P(None, 'tp'), may hold values from -0.078125 to 0.078125
- block_list: int32 [32, 3], P('resp'), may hold values from 0 to 7, as said below
- lengths: int32 [16], P('resp'), may hold values from 128 to 512, as said below
Outputs:
- x_grad: bfloat16 [8192, 5120], P(('resp', 'tp'))
- prefix_kv_grad: float32 [2048, 2048], P('resp', 'tp')
- resp_kv_grad: float32 [8192, 2048], P('resp', 'tp')
The draws below stay inside these ranges and needn't reach their ends.
Inputs may be any that keep to these rules, and one draw needn't show every extreme that they name: `block_list`: each row lists 3 different prompt blocks. `lengths`: at least one response is 512 tokens long.
All inputs are finite; a program needn't handle non-finite values.
Results may differ from the reference program's by a relative error of at most 0.02.
Values may be sent and summed in bfloat16 or wider, within the bound.
A program may use at most 128 MiB of HBM per device.

```python
import jax
import jax.numpy as jnp
from jax import lax

D = 5120
HEADS = 64
KVH = 8
HD = 128
RESP_DEV = 512
PREFIX = 2048
QBLK = 256
PBLK = 256
NBLK = 8
NSEL = 3
TOKENS = 8192
N_RESP = 16
N_TP = 8


def draw_queries(key, part):
    key = jax.random.fold_in(key, 11)
    base = jnp.clip(jax.random.normal(key, (TOKENS, HEADS, HD), jnp.float32), -6.0, 6.0)
    return base.reshape(TOKENS, HEADS * HD).astype(jnp.bfloat16)


def draw_prefix_kv(key, part):
    key = jax.random.fold_in(key, 12)
    base = jnp.clip(jax.random.normal(key, (PREFIX, KVH, 2, HD), jnp.float32), -6.0, 6.0)
    return base.reshape(PREFIX, KVH * 2 * HD).astype(jnp.bfloat16)


def draw_block_list(key, part):
    key = jax.random.fold_in(key, 13)
    row_keys = jax.random.split(key, TOKENS // QBLK)
    picked = jax.vmap(lambda row_key: jax.random.permutation(row_key, NBLK)[:NSEL])(row_keys)
    return picked.astype(jnp.int32)


def draw_lengths(key, part):
    key = jax.random.fold_in(key, 14)
    count = TOKENS // RESP_DEV
    drawn = jax.random.randint(key, (count,), RESP_DEV // 4, RESP_DEV + 1)
    longest = jax.random.randint(jax.random.fold_in(key, 1), (), 0, count)
    return jnp.where(jnp.arange(count) == longest, RESP_DEV, drawn).astype(jnp.int32)


def block_scale(key, shape, pieces, low, top_value):
    level, own = 1.0, jax.random.fold_in(key, 6)
    for dim, parts in pieces:
        draws = jnp.exp(jax.random.uniform(jax.random.fold_in(own, dim), (parts,), jnp.float32, low / len(pieces), top_value / len(pieces)))
        level = level * jnp.repeat(draws, shape[dim] // parts).reshape([-1 if axis == dim else 1 for axis in range(len(shape))])
    return level


def bell_draw(own_key, dims, scale, bound, cuts=(), held_as=jnp.bfloat16):
    entries = scale * jax.random.normal(own_key, dims, jnp.float32)
    if cuts:
        entries = entries * block_scale(own_key, dims, cuts, -0.22, 0.18)
    return jnp.clip(entries, -bound, bound).astype(held_as)


def setup_inputs(seed: int = 0) -> dict:
    splits = jax.random.split(jax.random.key(seed), 8)
    queries = draw_queries(jax.random.fold_in(splits[7], 71), 0)
    out_grad = bell_draw(splits[1], (TOKENS, HEADS * HD), 1.0, 6.0, ((0, 16), (1, 8)))
    resp_kv = bell_draw(splits[2], (TOKENS, KVH * 2 * HD), 1.0, 6.0, ((0, 16), (1, 8)))
    prefix_kv = draw_prefix_kv(jax.random.fold_in(splits[7], 71), 0)
    q_weight = bell_draw(splits[4], (D, HEADS * HD), D ** -0.5, 0.078125, ((1, 8),))
    block_list = draw_block_list(jax.random.fold_in(splits[7], 71), 0)
    lengths = draw_lengths(jax.random.fold_in(splits[7], 71), 0)
    return {"queries": queries, "out_grad": out_grad, "resp_kv": resp_kv, "prefix_kv": prefix_kv, "q_weight": q_weight, "block_list": block_list, "lengths": lengths}


def widen(values):
    return lax.optimization_barrier(values).astype(jnp.float32)


def block_grads(query_block, grad_block, keys, values, allowed):
    softmax_scale = HD ** -0.5
    query_wide = query_block.astype(jnp.float32)
    grad_wide = grad_block.astype(jnp.float32)
    key_wide = keys.astype(jnp.float32)
    value_wide = values.astype(jnp.float32)
    scores = jnp.einsum("qcgd,kcd->cgqk", query_wide, key_wide) * softmax_scale
    scores = jnp.where(allowed, scores, -jnp.inf)
    row_max = jnp.max(scores, axis=-1, keepdims=True)
    exponents = jnp.exp(scores - row_max)
    weights = exponents / jnp.sum(exponents, axis=-1, keepdims=True)
    weights_low = widen(weights.astype(jnp.bfloat16))
    attended = jnp.einsum("cgqk,kcd->qcgd", weights_low, value_wide)
    row_delta = jnp.transpose(jnp.sum(grad_wide * attended, axis=-1), (1, 2, 0))[..., None]
    weight_grad = jnp.einsum("qcgd,kcd->cgqk", grad_wide, value_wide)
    score_grad = widen((weights * (weight_grad - row_delta)).astype(jnp.bfloat16))
    query_grad = jnp.einsum("cgqk,kcd->qcgd", score_grad, key_wide) * softmax_scale
    key_grad = jnp.einsum("cgqk,qcgd->kcd", score_grad, query_wide) * softmax_scale
    value_grad = jnp.einsum("cgqk,qcgd->kcd", weights_low, grad_wide)
    return query_grad, jnp.stack([key_grad, value_grad], axis=2)


def reference(queries, out_grad, resp_kv, prefix_kv, q_weight, block_list, lengths):
    group_size = HEADS // KVH
    position = jnp.arange(RESP_DEV, dtype=jnp.int32)
    prefix_blocks = prefix_kv.reshape(PREFIX // PBLK, PBLK, KVH, 2, HD)
    query_all = queries.reshape(N_RESP, RESP_DEV, KVH, group_size, HD)
    grad_all = out_grad.reshape(N_RESP, RESP_DEV, KVH, group_size, HD)
    own_all = resp_kv.reshape(N_RESP, RESP_DEV, KVH, 2, HD)
    lists_all = block_list.reshape(N_RESP, RESP_DEV // QBLK, NSEL)

    def one_response(prefix_acc, inputs):
        query_heads, grad_heads, own_kv, lists, length = inputs
        live_rows = position < length
        grad_heads = jnp.where(live_rows[:, None, None, None], grad_heads, jnp.zeros_like(grad_heads))
        own_acc = jnp.zeros(own_kv.shape, jnp.float32)
        query_parts = []
        for block_index in range(RESP_DEV // QBLK):
            first_row = block_index * QBLK
            last_row = first_row + QBLK
            listed = lists[block_index].astype(jnp.int32)
            chosen = jnp.take(prefix_blocks, listed, axis=0).reshape(NSEL * PBLK, KVH, 2, HD)
            joined = jnp.concatenate([chosen, own_kv[:last_row]], axis=0)
            causal = position[:last_row][None, :] <= position[first_row:last_row][:, None]
            allowed = jnp.concatenate([jnp.ones((QBLK, NSEL * PBLK), bool), causal], axis=1)
            query_grad, kv_grad = block_grads(query_heads[first_row:last_row], grad_heads[first_row:last_row], joined[:, :, 0], joined[:, :, 1], allowed)
            query_parts.append(query_grad)
            prefix_acc = prefix_acc.at[listed].add(kv_grad[:NSEL * PBLK].reshape(NSEL, PBLK, KVH, 2, HD))
            own_acc = own_acc.at[:last_row].add(kv_grad[NSEL * PBLK:])
        query_grad = jnp.concatenate(query_parts, axis=0).reshape(RESP_DEV, HEADS * HD).astype(jnp.bfloat16)
        return prefix_acc, (query_grad, own_acc.reshape(RESP_DEV, KVH * 2 * HD))

    start_acc = jnp.zeros(prefix_blocks.shape, jnp.float32)
    prefix_acc, outputs = lax.scan(one_response, start_acc, (query_all, grad_all, own_all, lists_all, lengths))
    query_grad = outputs[0].reshape(TOKENS, HEADS * HD)
    own_grad = outputs[1].reshape(TOKENS, KVH * 2 * HD)
    group_width = HEADS * HD // N_TP
    input_total = jnp.zeros((TOKENS, D), jnp.float32)
    for group_index in range(N_TP):
        low_col = group_index * group_width
        high_col = low_col + group_width
        product = jnp.dot(query_grad[:, low_col:high_col], q_weight[:, low_col:high_col].T, preferred_element_type=jnp.float32)
        input_total = input_total + widen(product.astype(jnp.bfloat16))
    return input_total.astype(jnp.bfloat16), prefix_acc.reshape(PREFIX, KVH * 2 * HD), own_grad
```

```python
import functools

import jax
import jax.numpy as jnp
from jax import lax
from jax.experimental import pallas as pl
from jax.experimental.pallas import tpu as pltpu
from jax.sharding import PartitionSpec as P

HD = 128
QB = 256
NSEL = 3
HEADS_L = 8
SCALE = HD ** (-0.5)
EXP2_SCALE = SCALE * 1.4426950408889634
ROWS = 64
CC = 512
NX = 4
NY = 6
MESH = pl.DeviceIdType.MESH
BF = jnp.bfloat16
F32 = jnp.float32
NN = (((1,), (0,)), ((), ()))
NT = (((1,), (1,)), ((), ()))
TN = (((0,), (0,)), ((), ()))


def mm(a, b, dims):
    return lax.dot_general(a, b, dims, preferred_element_type=F32)


def attend(i, length, q_ref, do_ref, kv_ref, acck, accv, dqs):
    n = NSEL + i + 1
    r0 = i * QB
    live = (lax.broadcasted_iota(jnp.int32, (QB, 1), 0) + r0) < length

    def head(h, first):
        hs = pl.ds(pl.multiple_of(h * HD, HD), HD)
        q = q_ref[pl.ds(r0, QB), hs]
        do = jnp.where(live, do_ref[pl.ds(r0, QB), hs], jnp.zeros((), BF))
        scores = []
        for j in range(n):
            s = mm(kv_ref[pl.ds(j * QB, QB), :HD], q, NT)
            if j == n - 1:
                key_pos = lax.broadcasted_iota(jnp.int32, (QB, QB), 0)
                query_pos = lax.broadcasted_iota(jnp.int32, (QB, QB), 1)
                s = jnp.where(key_pos <= query_pos, s, -jnp.inf)
            scores.append(s)
        top = functools.reduce(jnp.maximum, [jnp.max(s, axis=0, keepdims=True) for s in scores])
        exps = [jnp.exp2((s - top) * EXP2_SCALE) for s in scores]
        total = functools.reduce(jnp.add, [jnp.sum(e, axis=0, keepdims=True) for e in exps])
        inverse = 1.0 / total
        weights = [e * inverse for e in exps]
        wgrads = [mm(kv_ref[pl.ds(j * QB, QB), HD:], do, NT) for j in range(n)]
        delta = functools.reduce(
            jnp.add, [jnp.sum(p * d, axis=0, keepdims=True) for p, d in zip(weights, wgrads)]
        )
        dq = None
        for j in range(n):
            ks = pl.ds(j * QB, QB)
            low = weights[j].astype(BF)
            ds = (weights[j] * (wgrads[j] - delta)).astype(BF)
            dv = mm(low, do, NN)
            dk = mm(ds, q, NN)
            if first:
                accv[ks, :] = dv
                acck[ks, :] = dk
            else:
                accv[ks, :] += dv
                acck[ks, :] += dk
            term = mm(ds, kv_ref[ks, :HD], TN)
            dq = term if dq is None else dq + term
        dqs[pl.ds(r0, QB), hs] = (dq * SCALE).astype(BF)

    head(0, True)

    def body(h, carry):
        head(h, False)
        return carry

    lax.fori_loop(1, HEADS_L, body, 0)


def kernel(
    q_hbm, do_hbm, rkv, pkv, w_hbm, blocks, lengths,
    x_out, pg_out, rg_out,
    qv, dov, wv, kvg, kvs, acck, accv, dqs,
    part_x, part_y, x1_buf, y1_buf, x2_buf, y2_buf, pp, p0_buf, p1_buf,
    load_sem, ag_s, ag_r, cg_s, cg_r,
    x1_s, x1_r, y1_s, y1_r, x2_s, x2_r, y2_s, y2_r, p0_s, p0_r, p1_s, p1_r,
):
    r = lax.axis_index("resp")
    t = lax.axis_index("tp")
    core = r % 2
    chip = r // 2
    x = t // 2
    yh = t % 2
    other = 1 - yh

    def remote(src, dst, ss, rs, device):
        return pltpu.make_async_remote_copy(
            src_ref=src, dst_ref=dst, send_sem=ss, recv_sem=rs,
            device_id=device, device_id_type=MESH,
        )

    sibling = (chip * 2 + 1 - core, t)
    y_mate = (r, x * 2 + other)

    def x_mate(xp):
        return (r, xp * 2 + yh)

    def chip_mate(cp):
        return (cp * 2 + core, t)

    loads = [
        pltpu.make_async_copy(q_hbm, qv, load_sem.at[0]),
        pltpu.make_async_copy(do_hbm, dov, load_sem.at[1]),
    ]
    w_loads = [pltpu.make_async_copy(w_hbm, wv, load_sem.at[2])]
    for copy in loads + w_loads:
        copy.start()

    barrier = pltpu.get_barrier_semaphore()
    mates = [sibling, y_mate]
    mates += [x_mate((x + d) % 4) for d in range(1, 4)]
    mates += [chip_mate((chip + k) % 8) for k in range(1, 8)]
    for mate in mates:
        pl.semaphore_signal(barrier, inc=1, device_id=mate, device_id_type=MESH)
    pl.semaphore_wait(barrier, len(mates))

    def prompt_rows(cp, c):
        return kvg.at[pl.ds(pl.multiple_of((cp * 2 + c) * 128, 128), 128), :]

    def ag_copy(to_chip, slot_chip):
        return remote(pkv, prompt_rows(slot_chip, core), ag_s.at[to_chip], ag_r.at[slot_chip], chip_mate(to_chip))

    def cg_copy(cp, c):
        return remote(prompt_rows(cp, c), prompt_rows(cp, c), cg_s.at[cp], cg_r.at[cp], sibling)

    for k in range(1, 8):
        ag_copy((chip + k) % 8, chip).start()
    kvg[pl.ds(pl.multiple_of(r * 128, 128), 128), :] = pkv[...]
    cg_copy(chip, core).start()
    for copy in loads:
        copy.wait()
    for k in range(1, 8):
        src = (chip + 8 - k) % 8
        ag_copy(src, src).wait_recv()
        cg_copy(src, core).start()
    for k in range(8):
        cg_copy((chip + 8 - k) % 8, 1 - core).wait_recv()

    def x1_copy(ch, xp, slot):
        return remote(part_x.at[ch, xp], x1_buf.at[ch, slot], x1_s.at[ch, xp], x1_r.at[ch, slot], x_mate(xp))

    def y1_copy(ch, i):
        return remote(
            part_y.at[ch, other, pl.ds(2 * i, 2)], y1_buf.at[ch, pl.ds(2 * i, 2)],
            y1_s.at[ch, i], y1_r.at[ch, i], y_mate,
        )

    def x2_copy(ch, xp, slot):
        return remote(part_y.at[ch, yh, xp], x2_buf.at[ch, slot], x2_s.at[ch, xp], x2_r.at[ch, slot], x_mate(xp))

    def y2_copy(ch):
        return remote(part_x.at[ch, x, other], y2_buf.at[ch], y2_s.at[ch], y2_r.at[ch], y_mate)

    def project(i, first_col):
        rows = dqs[pl.ds(pl.multiple_of(i * QB, QB), QB), :]
        cols = wv[pl.ds(pl.multiple_of(first_col, CC), CC), :]
        return mm(rows, cols, NT).astype(BF)

    def step(s, carry):
        i = (s + core) % 2

        for b in range(2):
            @pl.when(i == b)
            def _():
                for j in range(NSEL):
                    listed = jnp.full((QB, 2 * HD), blocks[b, j], jnp.int32)
                    chosen = kvg[pl.ds(0, QB), :]
                    for p in range(1, 8):
                        chosen = jnp.where(listed == p, kvg[pl.ds(p * QB, QB), :], chosen)
                    kvs[pl.ds(j * QB, QB), :] = chosen
                own = (b + 1) * QB
                kvs[pl.ds(NSEL * QB, own), :] = rkv[pl.ds(0, own), :]
                attend(b, lengths[0], qv, dov, kvs, acck.at[b], accv.at[b], dqs)

        @pl.when(s == 0)
        def _():
            for copy in w_loads:
                copy.wait()

        def chunk_x(ch, c):
            out = project(i, ch * CC)
            for k in range(4):
                part_x[ch, 2 * i + k // 2, k % 2] = out[k * ROWS:(k + 1) * ROWS]
            for d in range(1, 4):
                xp = (x + d) % 4
                @pl.when(xp // 2 == i)
                def _():
                    x1_copy(ch, xp, x).start()
            return c

        def chunk_y(ch, c):
            out = project(i, (NX + ch) * CC)
            for k in range(4):
                part_y[ch, k % 2, 2 * i + k // 2] = out[k * ROWS:(k + 1) * ROWS]
            y1_copy(ch, i).start()
            return c

        lax.fori_loop(0, NX, chunk_x, 0)
        lax.fori_loop(0, NY, chunk_y, 0)
        return carry

    lax.fori_loop(0, 2, step, 0)

    def prompt_sum(b, carry):
        sum_k = jnp.zeros((QB, HD), F32)
        sum_v = jnp.zeros((QB, HD), F32)
        for i in range(2):
            for j in range(NSEL):
                hit = jnp.full((QB, HD), blocks[i, j], jnp.int32) == b
                sum_k += jnp.where(hit, acck[i, pl.ds(j * QB, QB), :], 0.0)
                sum_v += jnp.where(hit, accv[i, pl.ds(j * QB, QB), :], 0.0)
        both = jnp.concatenate([sum_k * SCALE, sum_v], axis=1).astype(BF)
        pp[0, b] = both[:128]
        pp[1, b] = both[128:]
        return carry

    lax.fori_loop(0, 8, prompt_sum, 0)
    p0_copy = remote(pp.at[1 - core], p0_buf, p0_s.at[0], p0_r.at[0], sibling)
    p0_copy.start()

    def p1_copy(to_chip, slot):
        return remote(pp.at[core, to_chip], p1_buf.at[slot], p1_s.at[to_chip], p1_r.at[slot], chip_mate(to_chip))

    own0 = pl.ds(NSEL * QB, QB)
    own1 = pl.ds((NSEL + 1) * QB, QB)
    rg_out[pl.ds(0, QB), :HD] = (acck[0, own0, :] + acck[1, own0, :]) * SCALE
    rg_out[pl.ds(0, QB), HD:] = accv[0, own0, :] + accv[1, own0, :]
    rg_out[pl.ds(QB, QB), :HD] = acck[1, own1, :] * SCALE
    rg_out[pl.ds(QB, QB), HD:] = accv[1, own1, :]

    p0_copy.wait()

    def p_add(b, carry):
        pp[core, b] = (pp[core, b].astype(F32) + p0_buf[b].astype(F32)).astype(BF)
        return carry

    lax.fori_loop(0, 8, p_add, 0)
    for k in range(1, 8):
        p1_copy((chip + k) % 8, chip).start()

    def second(s, carry):
        i = (s + core) % 2

        def second_y(ch, c):
            y1_copy(ch, i).wait_recv()
            for k in range(2):
                xp = 2 * i + k
                part_y[ch, yh, xp] = (part_y[ch, yh, xp].astype(F32) + y1_buf[ch, xp].astype(F32)).astype(BF)
                @pl.when(xp != x)
                def _():
                    x2_copy(ch, xp, x).start()
            return c

        def second_x(ch, c):
            acc = part_x[ch, x, other].astype(F32)
            for d in range(1, 4):
                src = (x + d) % 4
                x1_copy(ch, src, src).wait_recv()
                acc += x1_buf[ch, src, other].astype(F32)
            part_x[ch, x, other] = acc.astype(BF)
            y2_copy(ch).start()
            return c

        @pl.when(x // 2 == i)
        def _():
            lax.fori_loop(0, NX, second_x, 0)

        lax.fori_loop(0, NY, second_y, 0)
        return carry

    lax.fori_loop(0, 2, second, 0)

    total = pp[core, chip].astype(F32)
    for k in range(1, 8):
        src = (chip + 8 - k) % 8
        p1_copy(src, src).wait_recv()
        total += p1_buf[src].astype(F32)
    pg_out[...] = total

    def last_x(ch, c):
        y2_copy(ch).wait_recv()
        acc = part_x[ch, x, yh].astype(F32) + y2_buf[ch].astype(F32)
        for d in range(1, 4):
            acc += x1_buf[ch, (x + d) % 4, yh].astype(F32)
        x_out[:, pl.ds(pl.multiple_of(ch * CC, CC), CC)] = acc.astype(BF)
        return c

    def last_y(ch, c):
        acc = part_y[ch, yh, x].astype(F32)
        for d in range(1, 4):
            src = (x + d) % 4
            x2_copy(ch, src, src).wait_recv()
            acc += x2_buf[ch, src].astype(F32)
        x_out[:, pl.ds(pl.multiple_of((NX + ch) * CC, CC), CC)] = acc.astype(BF)
        return c

    lax.fori_loop(0, NX, last_x, 0)
    lax.fori_loop(0, NY, last_y, 0)

    def sent_x(ch, c):
        for d in range(1, 4):
            x1_copy(ch, (x + d) % 4, x).wait_send()
        y2_copy(ch).wait_send()
        return c

    def sent_y(ch, c):
        for i in range(2):
            y1_copy(ch, i).wait_send()
        for d in range(1, 4):
            x2_copy(ch, (x + d) % 4, x).wait_send()
        return c

    lax.fori_loop(0, NX, sent_x, 0)
    lax.fori_loop(0, NY, sent_y, 0)
    for k in range(1, 8):
        ag_copy((chip + k) % 8, chip).wait_send()
        p1_copy((chip + k) % 8, chip).wait_send()
    for k in range(8):
        cg_copy((chip + 8 - k) % 8, core).wait_send()


def on_device(queries, out_grad, resp_kv, prefix_kv, q_weight, block_list, lengths):
    vmem = pl.BlockSpec(memory_space=pltpu.VMEM)
    smem = pl.BlockSpec(memory_space=pltpu.SMEM)
    hbm = pl.BlockSpec(memory_space=pl.ANY)
    dma = pltpu.SemaphoreType.DMA
    return pl.pallas_call(
        kernel,
        out_shape=(
            jax.ShapeDtypeStruct((ROWS, q_weight.shape[0]), BF),
            jax.ShapeDtypeStruct(prefix_kv.shape, F32),
            jax.ShapeDtypeStruct(resp_kv.shape, F32),
        ),
        in_specs=[hbm, hbm, vmem, vmem, hbm, smem, smem],
        out_specs=(vmem, vmem, vmem),
        scratch_shapes=[
            pltpu.VMEM(queries.shape, BF),
            pltpu.VMEM(out_grad.shape, BF),
            pltpu.VMEM(q_weight.shape, BF),
            pltpu.VMEM((2048, 256), BF),
            pltpu.VMEM((1280, 256), BF),
            pltpu.VMEM((2, 1280, HD), F32),
            pltpu.VMEM((2, 1280, HD), F32),
            pltpu.VMEM(queries.shape, BF),
            pltpu.VMEM((NX, 4, 2, ROWS, CC), BF),
            pltpu.VMEM((NY, 2, 4, ROWS, CC), BF),
            pltpu.VMEM((NX, 4, 2, ROWS, CC), BF),
            pltpu.VMEM((NY, 4, ROWS, CC), BF),
            pltpu.VMEM((NY, 4, ROWS, CC), BF),
            pltpu.VMEM((NX, ROWS, CC), BF),
            pltpu.VMEM((2, 8, 128, 256), BF),
            pltpu.VMEM((8, 128, 256), BF),
            pltpu.VMEM((8, 128, 256), BF),
            dma((3,)),
            dma((8,)), dma((8,)), dma((8,)), dma((8,)),
            dma((NX, 4)), dma((NX, 4)),
            dma((NY, 2)), dma((NY, 2)),
            dma((NY, 4)), dma((NY, 4)),
            dma((NX,)), dma((NX,)),
            dma((1,)), dma((1,)),
            dma((8,)), dma((8,)),
        ],
        compiler_params=pltpu.CompilerParams(
            collective_id=0, has_side_effects=True, vmem_limit_bytes=56 * 1024 * 1024
        ),
        cost_estimate=pl.CostEstimate(flops=12_000_000_000, bytes_accessed=16_000_000, transcendentals=5_000_000),
        name="attention_backward",
    )(queries, out_grad, resp_kv, prefix_kv, q_weight, block_list, lengths)


def solution(mesh):
    return jax.shard_map(
        on_device,
        mesh=mesh,
        in_specs=(
            P("resp", "tp"),
            P("resp", "tp"),
            P("resp", "tp"),
            P("resp", "tp"),
            P(None, "tp"),
            P("resp", None),
            P("resp"),
        ),
        out_specs=(P(("resp", "tp"), None), P("resp", "tp"), P("resp", "tp")),
        check_vma=False,
    )
```

```python
import functools

import jax
import jax.numpy as jnp
from jax import lax
from jax.experimental import pallas as pl
from jax.experimental.pallas import tpu as pltpu
from jax.sharding import PartitionSpec as P

HD = 128
QB = 256
NSEL = 3
HEADS_L = 8
SCALE = HD ** (-0.5)
EXP2_SCALE = SCALE * 1.4426950408889634
ROWS = 64
CC = 1024
NX = 2
NY = 3
CAT = 4
MESH = pl.DeviceIdType.MESH
BF = jnp.bfloat16
F32 = jnp.float32
NN = (((1,), (0,)), ((), ()))
NT = (((1,), (1,)), ((), ()))
TN = (((0,), (0,)), ((), ()))


def mm(a, b, dims):
    return lax.dot_general(a, b, dims, preferred_element_type=F32)


def attend(i, length, q_ref, do_ref, kv_ref, acck, accv, dqs):
    n = NSEL + i + 1
    keys = n * QB
    wide = CAT * QB
    r0 = i * QB
    live = (lax.broadcasted_iota(jnp.int32, (QB, 1), 0) + r0) < length
    all_keys = pl.ds(0, keys)
    keys_t = kv_ref[all_keys, :HD].T

    def group(g, first):
        slices = [pl.ds(pl.multiple_of((g * CAT + c) * HD, HD), HD) for c in range(CAT)]
        q = jnp.concatenate([q_ref[pl.ds(r0, QB), hs] for hs in slices], axis=0)
        do = jnp.concatenate(
            [jnp.where(live, do_ref[pl.ds(r0, QB), hs], jnp.zeros((), BF)) for hs in slices], axis=0
        )
        s = mm(kv_ref[all_keys, :HD], q, NT)
        scores = [s[j * QB:(j + 1) * QB] for j in range(n)]
        d = mm(kv_ref[all_keys, HD:], do, NT)
        wgrads = [d[j * QB:(j + 1) * QB] for j in range(n)]
        key_pos = lax.broadcasted_iota(jnp.int32, (QB, wide), 0)
        query_pos = lax.broadcasted_iota(jnp.int32, (QB, wide), 1) % QB
        scores[-1] = jnp.where(key_pos <= query_pos, scores[-1], -jnp.inf)
        top = functools.reduce(jnp.maximum, [jnp.max(s, axis=0, keepdims=True) for s in scores])
        exps = [jnp.exp2((s - top) * EXP2_SCALE) for s in scores]
        total = functools.reduce(jnp.add, [jnp.sum(e, axis=0, keepdims=True) for e in exps])
        inverse = 1.0 / total
        delta = inverse * functools.reduce(
            jnp.add, [jnp.sum(e * w, axis=0, keepdims=True) for e, w in zip(exps, wgrads)]
        )
        weights = [e * inverse for e in exps]
        low = jnp.concatenate([p.astype(BF) for p in weights], axis=0)
        ds = jnp.concatenate([(p * (w - delta)).astype(BF) for p, w in zip(weights, wgrads)], axis=0)
        dv = mm(low, do, NN)
        dk = mm(ds, q, NN)
        if first:
            accv[all_keys, :] = dv
            acck[all_keys, :] = dk
        else:
            accv[all_keys, :] += dv
            acck[all_keys, :] += dk
        dq = (mm(keys_t, ds, NN) * SCALE).T.astype(BF)
        for c, hs in enumerate(slices):
            dqs[pl.ds(r0, QB), hs] = dq[c * QB:(c + 1) * QB]

    group(0, True)

    def body(g, carry):
        group(g, False)
        return carry

    lax.fori_loop(1, HEADS_L // CAT, body, 0)


def kernel(
    q_hbm, do_hbm, rkv, pkv, w_hbm, blocks, lengths,
    x_out, pg_out, rg_out,
    qv, dov, wv, kvg, kvs, acck, accv, dqs,
    part_x, part_y, x1_buf, y1_buf, x2_buf, y2_buf, pp, p0_buf, p1_buf,
    load_sem, ag_s, ag_r, cg_s, cg_r,
    x1_s, x1_r, y1_s, y1_r, x2_s, x2_r, y2_s, y2_r, p0_s, p0_r, p1_s, p1_r,
):
    r = lax.axis_index("resp")
    t = lax.axis_index("tp")
    core = r % 2
    chip = r // 2
    x = t // 2
    yh = t % 2
    other = 1 - yh

    def remote(src, dst, ss, rs, device):
        return pltpu.make_async_remote_copy(
            src_ref=src, dst_ref=dst, send_sem=ss, recv_sem=rs,
            device_id=device, device_id_type=MESH,
        )

    sibling = (chip * 2 + 1 - core, t)
    y_mate = (r, x * 2 + other)

    def x_mate(xp):
        return (r, xp * 2 + yh)

    def chip_mate(cp):
        return (cp * 2 + core, t)

    loads = [
        pltpu.make_async_copy(q_hbm, qv, load_sem.at[0]),
        pltpu.make_async_copy(do_hbm, dov, load_sem.at[1]),
    ]
    w_loads = [pltpu.make_async_copy(w_hbm, wv, load_sem.at[2])]
    for copy in loads + w_loads:
        copy.start()

    barrier = pltpu.get_barrier_semaphore()
    mates = [sibling, y_mate]
    mates += [x_mate((x + d) % 4) for d in range(1, 4)]
    mates += [chip_mate((chip + k) % 8) for k in range(1, 8)]
    for mate in mates:
        pl.semaphore_signal(barrier, inc=1, device_id=mate, device_id_type=MESH)
    pl.semaphore_wait(barrier, len(mates))

    def prompt_rows(cp, c):
        return kvg.at[pl.ds(pl.multiple_of((cp * 2 + c) * 128, 128), 128), :]

    def ag_copy(to_chip, slot_chip):
        return remote(pkv, prompt_rows(slot_chip, core), ag_s.at[to_chip], ag_r.at[slot_chip], chip_mate(to_chip))

    def cg_copy(cp, c):
        return remote(prompt_rows(cp, c), prompt_rows(cp, c), cg_s.at[cp], cg_r.at[cp], sibling)

    for k in range(1, 8):
        ag_copy((chip + k) % 8, chip).start()
    kvg[pl.ds(pl.multiple_of(r * 128, 128), 128), :] = pkv[...]
    cg_copy(chip, core).start()
    for copy in loads:
        copy.wait()
    for k in range(1, 8):
        src = (chip + 8 - k) % 8
        ag_copy(src, src).wait_recv()
        cg_copy(src, core).start()
    for k in range(8):
        cg_copy((chip + 8 - k) % 8, 1 - core).wait_recv()

    def x1_copy(ch, xp, slot):
        return remote(part_x.at[ch, xp], x1_buf.at[ch, slot], x1_s.at[ch, xp], x1_r.at[ch, slot], x_mate(xp))

    def y1_copy(ch, i):
        return remote(
            part_y.at[ch, other, pl.ds(2 * i, 2)], y1_buf.at[ch, pl.ds(2 * i, 2)],
            y1_s.at[ch, i], y1_r.at[ch, i], y_mate,
        )

    def x2_copy(ch, xp, slot):
        return remote(part_y.at[ch, yh, xp], x2_buf.at[ch, slot], x2_s.at[ch, xp], x2_r.at[ch, slot], x_mate(xp))

    def y2_copy(ch):
        return remote(part_x.at[ch, x, other], y2_buf.at[ch], y2_s.at[ch], y2_r.at[ch], y_mate)

    def project(i, first_col):
        rows = dqs[pl.ds(pl.multiple_of(i * QB, QB), QB), :]
        cols = wv[pl.ds(pl.multiple_of(first_col, CC), CC), :]
        return mm(rows, cols, NT).astype(BF)

    def step(s, carry):
        i = (s + core) % 2

        for b in range(2):
            @pl.when(i == b)
            def _():
                for j in range(NSEL):
                    listed = jnp.full((QB, 2 * HD), blocks[b, j], jnp.int32)
                    chosen = kvg[pl.ds(0, QB), :]
                    for p in range(1, 8):
                        chosen = jnp.where(listed == p, kvg[pl.ds(p * QB, QB), :], chosen)
                    kvs[pl.ds(j * QB, QB), :] = chosen
                own = (b + 1) * QB
                kvs[pl.ds(NSEL * QB, own), :] = rkv[pl.ds(0, own), :]
                attend(b, lengths[0], qv, dov, kvs, acck.at[b], accv.at[b], dqs)

        @pl.when(s == 0)
        def _():
            for copy in w_loads:
                copy.wait()

        def chunk_x(ch, c):
            out = project(i, ch * CC)
            for k in range(4):
                part_x[ch, 2 * i + k // 2, k % 2] = out[k * ROWS:(k + 1) * ROWS]
            for d in range(1, 4):
                xp = (x + d) % 4
                @pl.when(xp // 2 == i)
                def _():
                    x1_copy(ch, xp, x).start()
            return c

        def chunk_y(ch, c):
            out = project(i, (NX + ch) * CC)
            for k in range(4):
                part_y[ch, k % 2, 2 * i + k // 2] = out[k * ROWS:(k + 1) * ROWS]
            y1_copy(ch, i).start()
            return c

        lax.fori_loop(0, NX, chunk_x, 0)
        lax.fori_loop(0, NY, chunk_y, 0)
        return carry

    lax.fori_loop(0, 2, step, 0)

    def prompt_sum(b, carry):
        sum_k = jnp.zeros((QB, HD), F32)
        sum_v = jnp.zeros((QB, HD), F32)
        for i in range(2):
            for j in range(NSEL):
                hit = jnp.full((QB, HD), blocks[i, j], jnp.int32) == b
                sum_k += jnp.where(hit, acck[i, pl.ds(j * QB, QB), :], 0.0)
                sum_v += jnp.where(hit, accv[i, pl.ds(j * QB, QB), :], 0.0)
        both = jnp.concatenate([sum_k * SCALE, sum_v], axis=1).astype(BF)
        pp[0, b] = both[:128]
        pp[1, b] = both[128:]
        return carry

    lax.fori_loop(0, 8, prompt_sum, 0)
    p0_copy = remote(pp.at[1 - core], p0_buf, p0_s.at[0], p0_r.at[0], sibling)
    p0_copy.start()

    def p1_copy(to_chip, slot):
        return remote(pp.at[core, to_chip], p1_buf.at[slot], p1_s.at[to_chip], p1_r.at[slot], chip_mate(to_chip))

    own0 = pl.ds(NSEL * QB, QB)
    own1 = pl.ds((NSEL + 1) * QB, QB)
    rg_out[pl.ds(0, QB), :HD] = (acck[0, own0, :] + acck[1, own0, :]) * SCALE
    rg_out[pl.ds(0, QB), HD:] = accv[0, own0, :] + accv[1, own0, :]
    rg_out[pl.ds(QB, QB), :HD] = acck[1, own1, :] * SCALE
    rg_out[pl.ds(QB, QB), HD:] = accv[1, own1, :]

    p0_copy.wait()

    def p_add(b, carry):
        pp[core, b] = (pp[core, b].astype(F32) + p0_buf[b].astype(F32)).astype(BF)
        return carry

    lax.fori_loop(0, 8, p_add, 0)
    for k in range(1, 8):
        p1_copy((chip + k) % 8, chip).start()

    def second(s, carry):
        i = (s + core) % 2

        def second_y(ch, c):
            y1_copy(ch, i).wait_recv()
            for k in range(2):
                xp = 2 * i + k
                part_y[ch, yh, xp] = (part_y[ch, yh, xp].astype(F32) + y1_buf[ch, xp].astype(F32)).astype(BF)
                @pl.when(xp != x)
                def _():
                    x2_copy(ch, xp, x).start()
            return c

        def second_x(ch, c):
            acc = part_x[ch, x, other].astype(F32)
            for d in range(1, 4):
                src = (x + d) % 4
                x1_copy(ch, src, src).wait_recv()
                acc += x1_buf[ch, src, other].astype(F32)
            part_x[ch, x, other] = acc.astype(BF)
            y2_copy(ch).start()
            return c

        @pl.when(x // 2 == i)
        def _():
            lax.fori_loop(0, NX, second_x, 0)

        lax.fori_loop(0, NY, second_y, 0)
        return carry

    lax.fori_loop(0, 2, second, 0)

    total = pp[core, chip].astype(F32)
    for k in range(1, 8):
        src = (chip + 8 - k) % 8
        p1_copy(src, src).wait_recv()
        total += p1_buf[src].astype(F32)
    pg_out[...] = total

    def last_x(ch, c):
        y2_copy(ch).wait_recv()
        acc = part_x[ch, x, yh].astype(F32) + y2_buf[ch].astype(F32)
        for d in range(1, 4):
            acc += x1_buf[ch, (x + d) % 4, yh].astype(F32)
        x_out[:, pl.ds(pl.multiple_of(ch * CC, CC), CC)] = acc.astype(BF)
        return c

    def last_y(ch, c):
        acc = part_y[ch, yh, x].astype(F32)
        for d in range(1, 4):
            src = (x + d) % 4
            x2_copy(ch, src, src).wait_recv()
            acc += x2_buf[ch, src].astype(F32)
        x_out[:, pl.ds(pl.multiple_of((NX + ch) * CC, CC), CC)] = acc.astype(BF)
        return c

    lax.fori_loop(0, NX, last_x, 0)
    lax.fori_loop(0, NY, last_y, 0)

    def sent_x(ch, c):
        for d in range(1, 4):
            x1_copy(ch, (x + d) % 4, x).wait_send()
        y2_copy(ch).wait_send()
        return c

    def sent_y(ch, c):
        for i in range(2):
            y1_copy(ch, i).wait_send()
        for d in range(1, 4):
            x2_copy(ch, (x + d) % 4, x).wait_send()
        return c

    lax.fori_loop(0, NX, sent_x, 0)
    lax.fori_loop(0, NY, sent_y, 0)
    for k in range(1, 8):
        ag_copy((chip + k) % 8, chip).wait_send()
        p1_copy((chip + k) % 8, chip).wait_send()
    for k in range(8):
        cg_copy((chip + 8 - k) % 8, core).wait_send()


def hand_over(*refs):
    count = len(refs) // 2
    sems = refs[-1]
    copies = [pltpu.make_async_copy(refs[k], refs[count + k], sems.at[k]) for k in range(count)]
    for copy in copies:
        copy.start()
    for copy in copies:
        copy.wait()


def on_device(queries, out_grad, resp_kv, prefix_kv, q_weight, block_list, lengths):
    vmem = pl.BlockSpec(memory_space=pltpu.VMEM)
    smem = pl.BlockSpec(memory_space=pltpu.SMEM)
    hbm = pl.BlockSpec(memory_space=pl.ANY)
    dma = pltpu.SemaphoreType.DMA
    results = pl.pallas_call(
        kernel,
        out_shape=(
            jax.ShapeDtypeStruct((ROWS, q_weight.shape[0]), BF),
            jax.ShapeDtypeStruct(prefix_kv.shape, F32),
            jax.ShapeDtypeStruct(resp_kv.shape, F32),
        ),
        in_specs=[hbm, hbm, vmem, vmem, hbm, smem, smem],
        out_specs=(vmem, vmem, vmem),
        scratch_shapes=[
            pltpu.VMEM(queries.shape, BF),
            pltpu.VMEM(out_grad.shape, BF),
            pltpu.VMEM(q_weight.shape, BF),
            pltpu.VMEM((2048, 256), BF),
            pltpu.VMEM((1280, 256), BF),
            pltpu.VMEM((2, 1280, HD), F32),
            pltpu.VMEM((2, 1280, HD), F32),
            pltpu.VMEM(queries.shape, BF),
            pltpu.VMEM((NX, 4, 2, ROWS, CC), BF),
            pltpu.VMEM((NY, 2, 4, ROWS, CC), BF),
            pltpu.VMEM((NX, 4, 2, ROWS, CC), BF),
            pltpu.VMEM((NY, 4, ROWS, CC), BF),
            pltpu.VMEM((NY, 4, ROWS, CC), BF),
            pltpu.VMEM((NX, ROWS, CC), BF),
            pltpu.VMEM((2, 8, 128, 256), BF),
            pltpu.VMEM((8, 128, 256), BF),
            pltpu.VMEM((8, 128, 256), BF),
            dma((3,)),
            dma((8,)), dma((8,)), dma((8,)), dma((8,)),
            dma((NX, 4)), dma((NX, 4)),
            dma((NY, 2)), dma((NY, 2)),
            dma((NY, 4)), dma((NY, 4)),
            dma((NX,)), dma((NX,)),
            dma((1,)), dma((1,)),
            dma((8,)), dma((8,)),
        ],
        compiler_params=pltpu.CompilerParams(
            collective_id=0, has_side_effects=True, vmem_limit_bytes=56 * 1024 * 1024
        ),
        cost_estimate=pl.CostEstimate(flops=12_000_000_000, bytes_accessed=16_000_000, transcendentals=5_000_000),
        name="attention_backward",
    )(queries, out_grad, resp_kv, prefix_kv, q_weight, block_list, lengths)
    return pl.pallas_call(
        hand_over,
        out_shape=tuple(jax.ShapeDtypeStruct(item.shape, item.dtype) for item in results),
        in_specs=[hbm] * 3,
        out_specs=(vmem, vmem, vmem),
        scratch_shapes=[dma((3,))],
        name="hand_over",
    )(*results)


def solution(mesh):
    return jax.shard_map(
        on_device,
        mesh=mesh,
        in_specs=(
            P("resp", "tp"),
            P("resp", "tp"),
            P("resp", "tp"),
            P("resp", "tp"),
            P(None, "tp"),
            P("resp", None),
            P("resp"),
        ),
        out_specs=(P(("resp", "tp"), None), P("resp", "tp"), P("resp", "tp")),
        check_vma=False,
    )
```

```python
import functools

import jax
import jax.numpy as jnp
from jax import lax
from jax.experimental import pallas as pl
from jax.experimental.pallas import tpu as pltpu
from jax.sharding import PartitionSpec as P

HD = 128
QB = 256
NSEL = 3
SCALE = HD ** (-0.5)
EXP2_SCALE = SCALE * 1.4426950408889634
ROWS = 64
QUARTER = 128
CC = 512
NC = 5
EARLY = 3
MESH = pl.DeviceIdType.MESH
BF = jnp.bfloat16
F32 = jnp.float32
NN = (((1,), (0,)), ((), ()))
NT = (((1,), (1,)), ((), ()))
TN = (((0,), (0,)), ((), ()))


def mm(a, b, dims):
    return lax.dot_general(a, b, dims, preferred_element_type=F32)


def attend(k, length, q_ref, do_ref, kv_ref, acck, accv, dqs):
    heads = q_ref.shape[1] // HD
    wide = heads * QUARTER
    r0 = k * QUARTER
    keys = NSEL * QB + r0 + QUARTER
    rows = pl.ds(r0, QUARTER)
    seen = pl.ds(0, keys)
    live = (lax.broadcasted_iota(jnp.int32, (QUARTER, 1), 0) + r0) < length
    slices = [pl.ds(h * HD, HD) for h in range(heads)]
    q = jnp.concatenate([q_ref[rows, hs] for hs in slices], axis=0)
    do = jnp.concatenate([jnp.where(live, do_ref[rows, hs], jnp.zeros((), BF)) for hs in slices], axis=0)
    cuts = [(c, c + QUARTER) for c in range(0, keys, QUARTER)]
    s = mm(kv_ref[seen, :HD], q, NT)
    scores = [s[low:high] for low, high in cuts]
    d = mm(kv_ref[seen, HD:], do, NT)
    wgrads = [d[low:high] for low, high in cuts]
    key_pos = lax.broadcasted_iota(jnp.int32, (QUARTER, wide), 0)
    query_pos = lax.broadcasted_iota(jnp.int32, (QUARTER, wide), 1) % QUARTER
    scores[-1] = jnp.where(key_pos <= query_pos, scores[-1], -jnp.inf)
    top = functools.reduce(jnp.maximum, [jnp.max(item, axis=0, keepdims=True) for item in scores])
    exps = [jnp.exp2((item - top) * EXP2_SCALE) for item in scores]
    total = functools.reduce(jnp.add, [jnp.sum(e, axis=0, keepdims=True) for e in exps])
    inverse = 1.0 / total
    delta = inverse * functools.reduce(
        jnp.add, [jnp.sum(e * w, axis=0, keepdims=True) for e, w in zip(exps, wgrads)]
    )
    weights = [e * inverse for e in exps]
    low = jnp.concatenate([p.astype(BF) for p in weights], axis=0)
    ds = jnp.concatenate([(p * (w - delta)).astype(BF) for p, w in zip(weights, wgrads)], axis=0)
    dv = mm(low, do, NN)
    dk = mm(ds, q, NN)
    if k % 2 == 0:
        rest = pl.ds(keys, QUARTER)
        accv[seen, :] = dv
        acck[seen, :] = dk
        accv[rest, :] = jnp.zeros((QUARTER, HD), F32)
        acck[rest, :] = jnp.zeros((QUARTER, HD), F32)
    else:
        accv[seen, :] += dv
        acck[seen, :] += dk
    dq = (mm(kv_ref[seen, :HD].T, ds, NN) * SCALE).T.astype(BF)
    for h, hs in enumerate(slices):
        dqs[pl.ds((k % 2) * QUARTER, QUARTER), hs] = dq[h * QUARTER:(h + 1) * QUARTER]


def kernel(
    q_hbm, do_hbm, rkv, pkv, w_hbm, blocks, lengths,
    x_out, pg_out, rg_out,
    qv, dov, wv, kvg, kvs, acck, accv, dqs,
    part_x, part_y, relay_buf, x1_buf, y1_buf, x2_buf, y2_buf, pp, p0_buf, p1_buf, p2_buf,
    load_sem, ag_s, ag_r, cg_s, cg_r, relay_s, relay_r,
    x1_s, x1_r, y1_s, y1_r, x2_s, x2_r, y2_s, y2_r, p0_s, p0_r, p1_s, p1_r, p2_s, p2_r,
):
    r = lax.axis_index("resp")
    t = lax.axis_index("tp")
    core = r % 2
    chip = r // 2
    y_lo = chip // 4
    z = chip % 4
    x = t // 2
    yh = t % 2
    other = 1 - yh
    after = (x + 1) % 4
    before = (x + 3) % 4
    across = (x + 2) % 4

    def remote(src, dst, ss, rs, device):
        return pltpu.make_async_remote_copy(
            src_ref=src, dst_ref=dst, send_sem=ss, recv_sem=rs,
            device_id=device, device_id_type=MESH,
        )

    sibling = (chip * 2 + 1 - core, t)
    y_mate = (r, x * 2 + other)

    def x_mate(xp):
        return (r, xp * 2 + yh)

    def chip_at(dy, dz):
        return ((y_lo + dy) % 2) * 4 + (z + dz) % 4

    def chip_mate(cp):
        return (cp * 2 + core, t)

    steps = [(0, 1), (0, 3), (1, 0), (0, 2), (1, 1), (1, 3), (1, 2)]

    loads = [
        pltpu.make_async_copy(q_hbm, qv, load_sem.at[0]),
        pltpu.make_async_copy(do_hbm, dov, load_sem.at[1]),
    ]
    w_loads = [pltpu.make_async_copy(w_hbm, wv, load_sem.at[2])]
    for copy in loads + w_loads:
        copy.start()

    barrier = pltpu.get_barrier_semaphore()
    mates = [sibling, y_mate, x_mate(after), x_mate(across), x_mate(before)]
    mates += [chip_mate(chip_at(dy, dz)) for dy, dz in steps]
    for mate in mates:
        pl.semaphore_signal(barrier, inc=1, device_id=mate, device_id_type=MESH)
    pl.semaphore_wait(barrier, len(mates))

    def prompt_rows(cp, c):
        return kvg.at[pl.ds(pl.multiple_of((cp * 2 + c) * 128, 128), 128), :]

    def ag_copy(to_chip, slot_chip):
        return remote(pkv, prompt_rows(slot_chip, core), ag_s.at[to_chip], ag_r.at[slot_chip], chip_mate(to_chip))

    def cg_copy(cp, c):
        return remote(prompt_rows(cp, c), prompt_rows(cp, c), cg_s.at[cp], cg_r.at[cp], sibling)

    for dy, dz in steps[::-1]:
        ag_copy(chip_at(dy, dz), chip).start()
    kvg[pl.ds(pl.multiple_of(r * 128, 128), 128), :] = pkv[...]
    cg_copy(chip, core).start()
    for copy in loads:
        copy.wait()
    for dy, dz in steps:
        src = chip_at(dy, dz)
        ag_copy(src, src).wait_recv()
        cg_copy(src, core).start()
    for dy, dz in [(0, 0)] + steps:
        cg_copy(chip_at(dy, dz), 1 - core).wait_recv()

    def relay_copy(ch, side):
        return remote(
            part_x.at[ch, across, side], relay_buf.at[ch, side], relay_s.at[ch, side], relay_r.at[ch, side],
            x_mate(after if side == 0 else before),
        )

    def x1_copy(ch, side, half):
        to = after if side == 0 else before
        return remote(
            part_x.at[ch, to, half], x1_buf.at[ch, side, half], x1_s.at[ch, side, half], x1_r.at[ch, side, half],
            x_mate(to),
        )

    def y1_copy(ch, i):
        pair = pl.ds(2 * i, 2)
        return remote(part_y.at[ch, other, pair], y1_buf.at[ch, pair], y1_s.at[ch, i], y1_r.at[ch, i], y_mate)

    def x2_copy(ch, xp, slot):
        return remote(part_y.at[ch, yh, xp], x2_buf.at[ch, slot], x2_s.at[ch, xp], x2_r.at[ch, slot], x_mate(xp))

    def y2_copy(ch):
        return remote(part_x.at[ch, x, other], y2_buf.at[ch], y2_s.at[ch], y2_r.at[ch], y_mate)

    def each_chunk(body, first=0, last=NC):
        def run(ch, carry):
            body(ch)
            return carry

        lax.fori_loop(first, last, run, 0)

    def project(i):
        def body(ch):
            cols = wv[pl.ds(pl.multiple_of(ch * 2 * CC, 2 * CC), 2 * CC), :]
            out = mm(dqs[...], cols, NT).astype(BF)
            for n in range(4):
                part_x[ch, 2 * i + n // 2, n % 2] = out[n * ROWS:(n + 1) * ROWS, :CC]
                part_y[ch, n % 2, 2 * i + n // 2] = out[n * ROWS:(n + 1) * ROWS, CC:]
            y1_copy(ch, i).start()

            @pl.when(across // 2 == i)
            def _():
                relay_copy(ch, 0).start()
                relay_copy(ch, 1).start()

            @pl.when(after // 2 == i)
            def _():
                x1_copy(ch, 0, 1).start()

            @pl.when(before // 2 == i)
            def _():
                x1_copy(ch, 1, 0).start()

        each_chunk(body)

    def pass_on(i):
        def body(ch):
            for side, to in ((0, after), (1, before)):
                @pl.when(to // 2 == i)
                def _():
                    relay_copy(ch, side).wait_recv()
                    mine = part_x[ch, to, side].astype(F32)
                    part_x[ch, to, side] = (mine + relay_buf[ch, side].astype(F32)).astype(BF)
                    x1_copy(ch, side, side).start()

        each_chunk(body)

    def second_y(i, first, last):
        def body(ch):
            y1_copy(ch, i).wait_recv()
            for n in range(2):
                k = 2 * i + n
                part_y[ch, yh, k] = (part_y[ch, yh, k].astype(F32) + y1_buf[ch, k].astype(F32)).astype(BF)

                @pl.when(k != x)
                def _():
                    x2_copy(ch, k, x).start()

        each_chunk(body, first, last)

    def second_x(i):
        def body(ch):
            acc = part_x[ch, x, other].astype(F32)
            for side in range(2):
                x1_copy(ch, side, other).wait_recv()
                acc += x1_buf[ch, side, other].astype(F32)
            part_x[ch, x, other] = acc.astype(BF)
            y2_copy(ch).start()

        @pl.when(x // 2 == i)
        def _():
            each_chunk(body)

    def step(s, carry):
        i = (s + core) % 2
        done = 1 - i

        for b in range(2):
            @pl.when(i == b)
            def _():
                for j in range(NSEL):
                    listed = jnp.full((QB, 2 * HD), blocks[b, j], jnp.int32)
                    chosen = kvg[pl.ds(0, QB), :]
                    for p in range(1, 8):
                        chosen = jnp.where(listed == p, kvg[pl.ds(p * QB, QB), :], chosen)
                    kvs[pl.ds(j * QB, QB), :] = chosen
                own = (b + 1) * QB
                kvs[pl.ds(NSEL * QB, own), :] = rkv[pl.ds(0, own), :]

        for n in range(2):
            for b in range(2):
                @pl.when(i == b)
                def _():
                    attend(2 * b + n, lengths[0], qv, dov, kvs, acck.at[b], accv.at[b], dqs)

            @pl.when(s == 1)
            def _():
                if n == 0:
                    pass_on(done)
                else:
                    second_y(done, 0, EARLY)
                    second_x(done)

        @pl.when(s == 0)
        def _():
            for copy in w_loads:
                copy.wait()

        project(i)
        return carry

    lax.fori_loop(0, 2, step, 0)
    first_half = core
    last_half = 1 - core
    second_y(first_half, EARLY, NC)

    def prompt_sum(b, carry):
        sum_k = jnp.zeros((QB, HD), F32)
        sum_v = jnp.zeros((QB, HD), F32)
        for i in range(2):
            for j in range(NSEL):
                hit = jnp.full((QB, HD), blocks[i, j], jnp.int32) == b
                sum_k += jnp.where(hit, acck[i, pl.ds(j * QB, QB), :], 0.0)
                sum_v += jnp.where(hit, accv[i, pl.ds(j * QB, QB), :], 0.0)
        both = jnp.concatenate([sum_k * SCALE, sum_v], axis=1).astype(BF)
        pp[0, b % 4, b // 4] = both[:128]
        pp[1, b % 4, b // 4] = both[128:]
        return carry

    lax.fori_loop(0, 8, prompt_sum, 0)
    p0_copy = remote(pp.at[1 - core], p0_buf, p0_s.at[0], p0_r.at[0], sibling)
    p0_copy.start()

    def p1_copy(zp, slot):
        return remote(pp.at[core, zp], p1_buf.at[slot], p1_s.at[zp], p1_r.at[slot], chip_mate(y_lo * 4 + zp))

    p2_copy = remote(pp.at[core, z, 1 - y_lo], p2_buf, p2_s.at[0], p2_r.at[0], chip_mate(chip_at(1, 0)))

    pass_on(last_half)

    p0_copy.wait()

    def p_add(b, carry):
        for half in range(2):
            pp[core, b, half] = (pp[core, b, half].astype(F32) + p0_buf[b, half].astype(F32)).astype(BF)
        return carry

    lax.fori_loop(0, 4, p_add, 0)
    for dz in (2, 1, 3):
        p1_copy((z + dz) % 4, z).start()

    own0 = pl.ds(NSEL * QB, QB)
    own1 = pl.ds((NSEL + 1) * QB, QB)
    rg_out[pl.ds(0, QB), :HD] = (acck[0, own0, :] + acck[1, own0, :]) * SCALE
    rg_out[pl.ds(0, QB), HD:] = accv[0, own0, :] + accv[1, own0, :]
    rg_out[pl.ds(QB, QB), :HD] = acck[1, own1, :] * SCALE
    rg_out[pl.ds(QB, QB), HD:] = accv[1, own1, :]

    second_y(last_half, 0, 3)
    second_x(last_half)
    second_y(last_half, 3, NC)

    for dz in (1, 3, 2):
        src = (z + dz) % 4
        p1_copy(src, src).wait_recv()
    for_mate = pp[core, z, 1 - y_lo].astype(F32)
    total = pp[core, z, y_lo].astype(F32)
    for dz in (1, 3, 2):
        for_mate += p1_buf[(z + dz) % 4, 1 - y_lo].astype(F32)
        total += p1_buf[(z + dz) % 4, y_lo].astype(F32)
    pp[core, z, 1 - y_lo] = for_mate.astype(BF)
    p2_copy.start()

    def last_x(ch):
        acc = part_x[ch, x, yh].astype(F32)
        for side in range(2):
            x1_copy(ch, side, yh).wait_recv()
            acc += x1_buf[ch, side, yh].astype(F32)
        y2_copy(ch).wait_recv()
        acc += y2_buf[ch].astype(F32)
        x_out[:, pl.ds(pl.multiple_of(ch * 2 * CC, 2 * CC), CC)] = acc.astype(BF)

    def last_y(ch):
        acc = part_y[ch, yh, x].astype(F32)
        for src in (after, before, across):
            x2_copy(ch, src, src).wait_recv()
            acc += x2_buf[ch, src].astype(F32)
        x_out[:, pl.ds(pl.multiple_of(ch * 2 * CC + CC, CC), CC)] = acc.astype(BF)

    each_chunk(last_x)
    p2_copy.wait()
    pg_out[...] = total + p2_buf[...].astype(F32)
    each_chunk(last_y)

    def sent(ch):
        for side in range(2):
            relay_copy(ch, side).wait_send()
            for half in range(2):
                x1_copy(ch, side, half).wait_send()
        y2_copy(ch).wait_send()
        for i in range(2):
            y1_copy(ch, i).wait_send()
        for xp in (after, before, across):
            x2_copy(ch, xp, x).wait_send()

    each_chunk(sent)
    for dy, dz in steps:
        ag_copy(chip_at(dy, dz), chip).wait_send()
    for dz in (1, 2, 3):
        p1_copy((z + dz) % 4, z).wait_send()
    for dy, dz in [(0, 0)] + steps:
        cg_copy(chip_at(dy, dz), core).wait_send()


def hand_over(*refs):
    count = len(refs) // 2
    sems = refs[-1]
    copies = [pltpu.make_async_copy(refs[k], refs[count + k], sems.at[k]) for k in range(count)]
    for copy in copies:
        copy.start()
    for copy in copies:
        copy.wait()


def on_device(queries, out_grad, resp_kv, prefix_kv, q_weight, block_list, lengths):
    vmem = pl.BlockSpec(memory_space=pltpu.VMEM)
    smem = pl.BlockSpec(memory_space=pltpu.SMEM)
    hbm = pl.BlockSpec(memory_space=pl.ANY)
    dma = pltpu.SemaphoreType.DMA
    results = pl.pallas_call(
        kernel,
        out_shape=(
            jax.ShapeDtypeStruct((ROWS, q_weight.shape[0]), BF),
            jax.ShapeDtypeStruct(prefix_kv.shape, F32),
            jax.ShapeDtypeStruct(resp_kv.shape, F32),
        ),
        in_specs=[hbm, hbm, vmem, vmem, hbm, smem, smem],
        out_specs=(vmem, vmem, vmem),
        scratch_shapes=[
            pltpu.VMEM(queries.shape, BF),
            pltpu.VMEM(out_grad.shape, BF),
            pltpu.VMEM(q_weight.shape, BF),
            pltpu.VMEM((2048, 256), BF),
            pltpu.VMEM((1280, 256), BF),
            pltpu.VMEM((2, 1280, HD), F32),
            pltpu.VMEM((2, 1280, HD), F32),
            pltpu.VMEM((QB, queries.shape[1]), BF),
            pltpu.VMEM((NC, 4, 2, ROWS, CC), BF),
            pltpu.VMEM((NC, 2, 4, ROWS, CC), BF),
            pltpu.VMEM((NC, 2, ROWS, CC), BF),
            pltpu.VMEM((NC, 2, 2, ROWS, CC), BF),
            pltpu.VMEM((NC, 4, ROWS, CC), BF),
            pltpu.VMEM((NC, 4, ROWS, CC), BF),
            pltpu.VMEM((NC, ROWS, CC), BF),
            pltpu.VMEM((2, 4, 2, 128, 256), BF),
            pltpu.VMEM((4, 2, 128, 256), BF),
            pltpu.VMEM((4, 2, 128, 256), BF),
            pltpu.VMEM((128, 256), BF),
            dma((3,)),
            dma((8,)), dma((8,)), dma((8,)), dma((8,)),
            dma((NC, 2)), dma((NC, 2)),
            dma((NC, 2, 2)), dma((NC, 2, 2)),
            dma((NC, 2)), dma((NC, 2)),
            dma((NC, 4)), dma((NC, 4)),
            dma((NC,)), dma((NC,)),
            dma((1,)), dma((1,)),
            dma((4,)), dma((4,)),
            dma((1,)), dma((1,)),
        ],
        compiler_params=pltpu.CompilerParams(
            collective_id=0, has_side_effects=True, vmem_limit_bytes=56 * 1024 * 1024
        ),
        cost_estimate=pl.CostEstimate(flops=12_000_000_000, bytes_accessed=16_000_000, transcendentals=5_000_000),
        name="attention_backward",
    )(queries, out_grad, resp_kv, prefix_kv, q_weight, block_list, lengths)
    return pl.pallas_call(
        hand_over,
        out_shape=tuple(jax.ShapeDtypeStruct(item.shape, item.dtype) for item in results),
        in_specs=[hbm] * 3,
        out_specs=(vmem, vmem, vmem),
        scratch_shapes=[dma((3,))],
        name="hand_over",
    )(*results)


def solution(mesh):
    return jax.shard_map(
        on_device,
        mesh=mesh,
        in_specs=(
            P("resp", "tp"),
            P("resp", "tp"),
            P("resp", "tp"),
            P("resp", "tp"),
            P(None, "tp"),
            P("resp", None),
            P("resp"),
        ),
        out_specs=(P(("resp", "tp"), None), P("resp", "tp"), P("resp", "tp")),
        check_vma=False,
    )
```

```python
import functools

import jax
import jax.numpy as jnp
from jax import lax
from jax.experimental import pallas as pl
from jax.experimental.pallas import tpu as pltpu
from jax.sharding import PartitionSpec as P

HD = 128
QB = 256
NSEL = 3
SCALE = HD ** (-0.5)
EXP2_SCALE = SCALE * 1.4426950408889634
ROWS = 64
QUARTER = 128
CX = 512
CY = 512
NC = 5
EARLY = 3
MESH = pl.DeviceIdType.MESH
BF = jnp.bfloat16
F32 = jnp.float32
NN = (((1,), (0,)), ((), ()))
NT = (((1,), (1,)), ((), ()))
TN = (((0,), (0,)), ((), ()))


def mm(a, b, dims):
    return lax.dot_general(a, b, dims, preferred_element_type=F32)


def attend(k, length, q_ref, do_ref, kv_ref, acck, accv, dqs):
    heads = q_ref.shape[1] // HD
    wide = heads * QUARTER
    r0 = k * QUARTER
    keys = NSEL * QB + r0 + QUARTER
    rows = pl.ds(r0, QUARTER)
    seen = pl.ds(0, keys)
    live = (lax.broadcasted_iota(jnp.int32, (QUARTER, 1), 0) + r0) < length
    slices = [pl.ds(h * HD, HD) for h in range(heads)]
    q = jnp.concatenate([q_ref[rows, hs] for hs in slices], axis=0)
    do = jnp.concatenate([jnp.where(live, do_ref[rows, hs], jnp.zeros((), BF)) for hs in slices], axis=0)
    cuts = [(c, c + QUARTER) for c in range(0, keys, QUARTER)]
    s = mm(kv_ref[seen, :HD], q, NT)
    scores = [s[low:high] for low, high in cuts]
    d = mm(kv_ref[seen, HD:], do, NT)
    wgrads = [d[low:high] for low, high in cuts]
    key_pos = lax.broadcasted_iota(jnp.int32, (QUARTER, wide), 0)
    query_pos = lax.broadcasted_iota(jnp.int32, (QUARTER, wide), 1) % QUARTER
    scores[-1] = jnp.where(key_pos <= query_pos, scores[-1], -jnp.inf)
    top = functools.reduce(jnp.maximum, [jnp.max(item, axis=0, keepdims=True) for item in scores])
    exps = [jnp.exp2((item - top) * EXP2_SCALE) for item in scores]
    total = functools.reduce(jnp.add, [jnp.sum(e, axis=0, keepdims=True) for e in exps])
    inverse = 1.0 / total
    delta = inverse * functools.reduce(
        jnp.add, [jnp.sum(e * w, axis=0, keepdims=True) for e, w in zip(exps, wgrads)]
    )
    weights = [e * inverse for e in exps]
    low = jnp.concatenate([p.astype(BF) for p in weights], axis=0)
    ds = jnp.concatenate([(p * (w - delta)).astype(BF) for p, w in zip(weights, wgrads)], axis=0)
    dv = mm(low, do, NN)
    dk = mm(ds, q, NN)
    if k % 2 == 0:
        rest = pl.ds(keys, QUARTER)
        accv[seen, :] = dv
        acck[seen, :] = dk
        accv[rest, :] = jnp.zeros((QUARTER, HD), F32)
        acck[rest, :] = jnp.zeros((QUARTER, HD), F32)
    else:
        accv[seen, :] += dv
        acck[seen, :] += dk
    dq = (mm(kv_ref[seen, :HD].T, ds, NN) * SCALE).T.astype(BF)
    for h, hs in enumerate(slices):
        dqs[pl.ds((k % 2) * QUARTER, QUARTER), hs] = dq[h * QUARTER:(h + 1) * QUARTER]


def kernel(
    q_hbm, do_hbm, rkv, pkv, w_hbm, blocks, lengths,
    x_hbm, pg_hbm, rg_hbm,
    x_out, pg_out, rg_out, out_sem,
    qv, dov, wv, kvg, kvs, acck, accv, dqs,
    part_x, part_y, relay_buf, x1_buf, y1_buf, x2_buf, y2_buf, pp, p0_buf, p1_buf, p2_buf,
    load_sem, ag_s, ag_r, cg_s, cg_r, relay_s, relay_r,
    x1_s, x1_r, y1_s, y1_r, x2_s, x2_r, y2_s, y2_r, p0_s, p0_r, p1_s, p1_r, p2_s, p2_r,
):
    r = lax.axis_index("resp")
    t = lax.axis_index("tp")
    core = r % 2
    chip = r // 2
    y_lo = chip // 4
    z = chip % 4
    x = t // 2
    yh = t % 2
    other = 1 - yh
    after = (x + 1) % 4
    before = (x + 3) % 4
    across = (x + 2) % 4

    def remote(src, dst, ss, rs, device):
        return pltpu.make_async_remote_copy(
            src_ref=src, dst_ref=dst, send_sem=ss, recv_sem=rs,
            device_id=device, device_id_type=MESH,
        )

    sibling = (chip * 2 + 1 - core, t)
    y_mate = (r, x * 2 + other)

    def x_mate(xp):
        return (r, xp * 2 + yh)

    def chip_at(dy, dz):
        return ((y_lo + dy) % 2) * 4 + (z + dz) % 4

    def chip_mate(cp):
        return (cp * 2 + core, t)

    steps = [(0, 1), (0, 3), (1, 0), (0, 2), (1, 1), (1, 3), (1, 2)]

    loads = [
        pltpu.make_async_copy(q_hbm, qv, load_sem.at[0]),
        pltpu.make_async_copy(do_hbm, dov, load_sem.at[1]),
    ]
    w_loads = [pltpu.make_async_copy(w_hbm, wv, load_sem.at[2])]
    for copy in loads + w_loads:
        copy.start()

    barrier = pltpu.get_barrier_semaphore()
    mates = [sibling, y_mate, x_mate(after), x_mate(across), x_mate(before)]
    mates += [chip_mate(chip_at(dy, dz)) for dy, dz in steps]
    for mate in mates:
        pl.semaphore_signal(barrier, inc=1, device_id=mate, device_id_type=MESH)
    pl.semaphore_wait(barrier, len(mates))

    def prompt_rows(cp, c):
        return kvg.at[pl.ds(pl.multiple_of((cp * 2 + c) * 128, 128), 128), :]

    def ag_copy(to_chip, slot_chip):
        return remote(pkv, prompt_rows(slot_chip, core), ag_s.at[to_chip], ag_r.at[slot_chip], chip_mate(to_chip))

    def cg_copy(cp, c):
        return remote(prompt_rows(cp, c), prompt_rows(cp, c), cg_s.at[cp], cg_r.at[cp], sibling)

    for dy, dz in steps:
        ag_copy(chip_at(dy, dz), chip).start()
    kvg[pl.ds(pl.multiple_of(r * 128, 128), 128), :] = pkv[...]
    cg_copy(chip, core).start()
    for copy in loads:
        copy.wait()
    for dy, dz in steps:
        src = chip_at(dy, dz)
        ag_copy(src, src).wait_recv()
        cg_copy(src, core).start()
    for dy, dz in [(0, 0)] + steps:
        cg_copy(chip_at(dy, dz), 1 - core).wait_recv()

    def relay_copy(ch, side):
        return remote(
            part_x.at[ch, across, side], relay_buf.at[ch, side], relay_s.at[ch, side], relay_r.at[ch, side],
            x_mate(after if side == 0 else before),
        )

    def x1_copy(ch, side, half):
        to = after if side == 0 else before
        return remote(
            part_x.at[ch, to, half], x1_buf.at[ch, side, half], x1_s.at[ch, side, half], x1_r.at[ch, side, half],
            x_mate(to),
        )

    def y1_copy(ch, i):
        pair = pl.ds(2 * i, 2)
        return remote(part_y.at[ch, other, pair], y1_buf.at[ch, pair], y1_s.at[ch, i], y1_r.at[ch, i], y_mate)

    def x2_copy(ch, xp, slot):
        return remote(part_y.at[ch, yh, xp], x2_buf.at[ch, slot], x2_s.at[ch, xp], x2_r.at[ch, slot], x_mate(xp))

    def y2_copy(ch):
        return remote(part_x.at[ch, x, other], y2_buf.at[ch], y2_s.at[ch], y2_r.at[ch], y_mate)

    def each_chunk(body, first=0, last=NC):
        def run(ch, carry):
            body(ch)
            return carry

        lax.fori_loop(first, last, run, 0)

    def project(i):
        def body(ch):
            cols = wv[pl.ds(pl.multiple_of(ch * (CX + CY), CX + CY), CX + CY), :]
            out = mm(dqs[...], cols, NT).astype(BF)
            for n in range(4):
                part_x[ch, 2 * i + n // 2, n % 2] = out[n * ROWS:(n + 1) * ROWS, :CX]
                part_y[ch, n % 2, 2 * i + n // 2] = out[n * ROWS:(n + 1) * ROWS, CX:]
            y1_copy(ch, i).start()

            @pl.when(across // 2 == i)
            def _():
                relay_copy(ch, 0).start()
                relay_copy(ch, 1).start()

            @pl.when(after // 2 == i)
            def _():
                x1_copy(ch, 0, 1).start()

            @pl.when(before // 2 == i)
            def _():
                x1_copy(ch, 1, 0).start()

        each_chunk(body)

    def pass_on(i):
        def body(ch):
            for side, to in ((0, after), (1, before)):
                @pl.when(to // 2 == i)
                def _():
                    relay_copy(ch, side).wait_recv()
                    mine = part_x[ch, to, side].astype(F32)
                    part_x[ch, to, side] = (mine + relay_buf[ch, side].astype(F32)).astype(BF)
                    x1_copy(ch, side, side).start()

        each_chunk(body)

    def second_y(i, first, last):
        def body(ch):
            y1_copy(ch, i).wait_recv()
            for n in range(2):
                k = 2 * i + n
                part_y[ch, yh, k] = (part_y[ch, yh, k].astype(F32) + y1_buf[ch, k].astype(F32)).astype(BF)

                @pl.when(k != x)
                def _():
                    x2_copy(ch, k, x).start()

        each_chunk(body, first, last)

    def second_x(i):
        def body(ch):
            acc = part_x[ch, x, other].astype(F32)
            for side in range(2):
                x1_copy(ch, side, other).wait_recv()
                acc += x1_buf[ch, side, other].astype(F32)
            part_x[ch, x, other] = acc.astype(BF)
            y2_copy(ch).start()

        @pl.when(x // 2 == i)
        def _():
            each_chunk(body)

    def step(s, carry):
        i = (s + core) % 2
        done = 1 - i

        for b in range(2):
            @pl.when(i == b)
            def _():
                for j in range(NSEL):
                    listed = jnp.full((QB, 2 * HD), blocks[b, j], jnp.int32)
                    chosen = kvg[pl.ds(0, QB), :]
                    for p in range(1, 8):
                        chosen = jnp.where(listed == p, kvg[pl.ds(p * QB, QB), :], chosen)
                    kvs[pl.ds(j * QB, QB), :] = chosen
                own = (b + 1) * QB
                kvs[pl.ds(NSEL * QB, own), :] = rkv[pl.ds(0, own), :]

        for n in range(2):
            for b in range(2):
                @pl.when(i == b)
                def _():
                    attend(2 * b + n, lengths[0], qv, dov, kvs, acck.at[b], accv.at[b], dqs)

            @pl.when(s == 1)
            def _():
                if n == 0:
                    pass_on(done)
                else:
                    second_y(done, 0, EARLY)
                    second_x(done)

        @pl.when(s == 0)
        def _():
            for copy in w_loads:
                copy.wait()

        project(i)
        return carry

    lax.fori_loop(0, 2, step, 0)
    first_half = core
    last_half = 1 - core
    second_y(first_half, EARLY, NC)

    def prompt_sum(b, carry):
        sum_k = jnp.zeros((QB, HD), F32)
        sum_v = jnp.zeros((QB, HD), F32)
        for i in range(2):
            for j in range(NSEL):
                hit = jnp.full((QB, HD), blocks[i, j], jnp.int32) == b
                sum_k += jnp.where(hit, acck[i, pl.ds(j * QB, QB), :], 0.0)
                sum_v += jnp.where(hit, accv[i, pl.ds(j * QB, QB), :], 0.0)
        both = jnp.concatenate([sum_k * SCALE, sum_v], axis=1).astype(BF)
        pp[0, b % 4, b // 4] = both[:128]
        pp[1, b % 4, b // 4] = both[128:]
        return carry

    lax.fori_loop(0, 8, prompt_sum, 0)
    p0_copy = remote(pp.at[1 - core], p0_buf, p0_s.at[0], p0_r.at[0], sibling)
    p0_copy.start()

    def p1_copy(zp, slot):
        return remote(pp.at[core, zp], p1_buf.at[slot], p1_s.at[zp], p1_r.at[slot], chip_mate(y_lo * 4 + zp))

    p2_copy = remote(pp.at[core, z, 1 - y_lo], p2_buf, p2_s.at[0], p2_r.at[0], chip_mate(chip_at(1, 0)))

    pass_on(last_half)

    p0_copy.wait()

    def p_add(b, carry):
        for half in range(2):
            pp[core, b, half] = (pp[core, b, half].astype(F32) + p0_buf[b, half].astype(F32)).astype(BF)
        return carry

    lax.fori_loop(0, 4, p_add, 0)
    for dz in (2, 1, 3):
        p1_copy((z + dz) % 4, z).start()

    own0 = pl.ds(NSEL * QB, QB)
    own1 = pl.ds((NSEL + 1) * QB, QB)
    rg_out[pl.ds(0, QB), :HD] = (acck[0, own0, :] + acck[1, own0, :]) * SCALE
    rg_out[pl.ds(0, QB), HD:] = accv[0, own0, :] + accv[1, own0, :]
    rg_out[pl.ds(QB, QB), :HD] = acck[1, own1, :] * SCALE
    rg_out[pl.ds(QB, QB), HD:] = accv[1, own1, :]
    rg_copy = pltpu.make_async_copy(rg_out, rg_hbm, out_sem.at[2 * NC])
    rg_copy.start()

    second_y(last_half, 0, 3)
    second_x(last_half)
    second_y(last_half, 3, NC)

    for dz in (1, 3, 2):
        src = (z + dz) % 4
        p1_copy(src, src).wait_recv()
    for_mate = pp[core, z, 1 - y_lo].astype(F32)
    total = pp[core, z, y_lo].astype(F32)
    for dz in (1, 3, 2):
        for_mate += p1_buf[(z + dz) % 4, 1 - y_lo].astype(F32)
        total += p1_buf[(z + dz) % 4, y_lo].astype(F32)
    pp[core, z, 1 - y_lo] = for_mate.astype(BF)
    p2_copy.start()

    def out_copy(ch, kind):
        start, size = ((0, CX), (CX, CY))[kind]
        cols = pl.ds(pl.multiple_of(ch * (CX + CY) + start, 128), size)
        return pltpu.make_async_copy(x_out.at[:, cols], x_hbm.at[:, cols], out_sem.at[2 * ch + kind])

    def last_x(ch):
        acc = part_x[ch, x, yh].astype(F32)
        for side in range(2):
            x1_copy(ch, side, yh).wait_recv()
            acc += x1_buf[ch, side, yh].astype(F32)
        y2_copy(ch).wait_recv()
        acc += y2_buf[ch].astype(F32)
        x_out[:, pl.ds(pl.multiple_of(ch * (CX + CY), 128), CX)] = acc.astype(BF)
        out_copy(ch, 0).start()

    def last_y(ch):
        acc = part_y[ch, yh, x].astype(F32)
        for src in (after, before, across):
            x2_copy(ch, src, src).wait_recv()
            acc += x2_buf[ch, src].astype(F32)
        x_out[:, pl.ds(pl.multiple_of(ch * (CX + CY) + CX, 128), CY)] = acc.astype(BF)
        out_copy(ch, 1).start()

    each_chunk(last_x)
    p2_copy.wait()
    pg_out[...] = total + p2_buf[...].astype(F32)
    pg_copy = pltpu.make_async_copy(pg_out, pg_hbm, out_sem.at[2 * NC + 1])
    pg_copy.start()
    each_chunk(last_y)

    def sent(ch):
        for side in range(2):
            relay_copy(ch, side).wait_send()
            for half in range(2):
                x1_copy(ch, side, half).wait_send()
        y2_copy(ch).wait_send()
        for kind in range(2):
            out_copy(ch, kind).wait()
        for i in range(2):
            y1_copy(ch, i).wait_send()
        for xp in (after, before, across):
            x2_copy(ch, xp, x).wait_send()

    each_chunk(sent)
    rg_copy.wait()
    pg_copy.wait()
    for dy, dz in steps:
        ag_copy(chip_at(dy, dz), chip).wait_send()
    for dz in (1, 2, 3):
        p1_copy((z + dz) % 4, z).wait_send()
    for dy, dz in [(0, 0)] + steps:
        cg_copy(chip_at(dy, dz), core).wait_send()


def hand_over(x_in, pg_in, rg_in, x_to, pg_to, rg_to, x_v, pg_v, rg_v, in_sem, out_sem):
    pieces = []
    for source, held, target, count in ((x_in, x_v, x_to, 4), (rg_in, rg_v, rg_to, 4), (pg_in, pg_v, pg_to, 1)):
        rows = source.shape[0] // count
        pieces += [(source, held, target, pl.ds(n * rows, rows)) for n in range(count)]
    ins = [pltpu.make_async_copy(s.at[c], v.at[c], in_sem.at[n]) for n, (s, v, _, c) in enumerate(pieces)]
    outs = [pltpu.make_async_copy(v.at[c], o.at[c], out_sem.at[n]) for n, (_, v, o, c) in enumerate(pieces)]
    for copy in ins:
        copy.start()
    for copy_in, copy_out in zip(ins, outs):
        copy_in.wait()
        copy_out.start()
    for copy in outs:
        copy.wait()


def on_device(queries, out_grad, resp_kv, prefix_kv, q_weight, block_list, lengths):
    vmem = pl.BlockSpec(memory_space=pltpu.VMEM)
    smem = pl.BlockSpec(memory_space=pltpu.SMEM)
    hbm = pl.BlockSpec(memory_space=pl.ANY)
    dma = pltpu.SemaphoreType.DMA
    results = pl.pallas_call(
        kernel,
        out_shape=(
            jax.ShapeDtypeStruct((ROWS, q_weight.shape[0]), BF),
            jax.ShapeDtypeStruct(prefix_kv.shape, F32),
            jax.ShapeDtypeStruct(resp_kv.shape, F32),
        ),
        in_specs=[hbm, hbm, vmem, vmem, hbm, smem, smem],
        out_specs=(hbm, hbm, hbm),
        scratch_shapes=[
            pltpu.VMEM((ROWS, q_weight.shape[0]), BF),
            pltpu.VMEM(prefix_kv.shape, F32),
            pltpu.VMEM(resp_kv.shape, F32),
            dma((2 + 2 * NC,)),
            pltpu.VMEM(queries.shape, BF),
            pltpu.VMEM(out_grad.shape, BF),
            pltpu.VMEM(q_weight.shape, BF),
            pltpu.VMEM((2048, 256), BF),
            pltpu.VMEM((1280, 256), BF),
            pltpu.VMEM((2, 1280, HD), F32),
            pltpu.VMEM((2, 1280, HD), F32),
            pltpu.VMEM((QB, queries.shape[1]), BF),
            pltpu.VMEM((NC, 4, 2, ROWS, CX), BF),
            pltpu.VMEM((NC, 2, 4, ROWS, CY), BF),
            pltpu.VMEM((NC, 2, ROWS, CX), BF),
            pltpu.VMEM((NC, 2, 2, ROWS, CX), BF),
            pltpu.VMEM((NC, 4, ROWS, CY), BF),
            pltpu.VMEM((NC, 4, ROWS, CY), BF),
            pltpu.VMEM((NC, ROWS, CX), BF),
            pltpu.VMEM((2, 4, 2, 128, 256), BF),
            pltpu.VMEM((4, 2, 128, 256), BF),
            pltpu.VMEM((4, 2, 128, 256), BF),
            pltpu.VMEM((128, 256), BF),
            dma((3,)),
            dma((8,)), dma((8,)), dma((8,)), dma((8,)),
            dma((NC, 2)), dma((NC, 2)),
            dma((NC, 2, 2)), dma((NC, 2, 2)),
            dma((NC, 2)), dma((NC, 2)),
            dma((NC, 4)), dma((NC, 4)),
            dma((NC,)), dma((NC,)),
            dma((1,)), dma((1,)),
            dma((4,)), dma((4,)),
            dma((1,)), dma((1,)),
        ],
        compiler_params=pltpu.CompilerParams(
            collective_id=0, has_side_effects=True, vmem_limit_bytes=56 * 1024 * 1024
        ),
        cost_estimate=pl.CostEstimate(flops=12_000_000_000, bytes_accessed=16_000_000, transcendentals=5_000_000),
        name="attention_backward",
    )(queries, out_grad, resp_kv, prefix_kv, q_weight, block_list, lengths)
    return pl.pallas_call(
        hand_over,
        out_shape=tuple(jax.ShapeDtypeStruct(item.shape, item.dtype) for item in results),
        in_specs=[hbm] * 3,
        out_specs=(hbm, hbm, hbm),
        scratch_shapes=[pltpu.VMEM(item.shape, item.dtype) for item in results] + [dma((9,)), dma((9,))],
        name="hand_over",
    )(*results)


def solution(mesh):
    return jax.shard_map(
        on_device,
        mesh=mesh,
        in_specs=(
            P("resp", "tp"),
            P("resp", "tp"),
            P("resp", "tp"),
            P("resp", "tp"),
            P(None, "tp"),
            P("resp", None),
            P("resp"),
        ),
        out_specs=(P(("resp", "tp"), None), P("resp", "tp"), P("resp", "tp")),
        check_vma=False,
    )
```

```python
import functools

import jax
import jax.numpy as jnp
from jax import lax
from jax.experimental import pallas as pl
from jax.experimental.pallas import tpu as pltpu
from jax.sharding import PartitionSpec as P

HD = 128
QB = 256
NSEL = 3
SCALE = HD ** (-0.5)
EXP2_SCALE = SCALE * 1.4426950408889634
ROWS = 64
QUARTER = 128
CX = 512
CY = 512
NC = 5
EARLY = 4
MESH = pl.DeviceIdType.MESH
BF = jnp.bfloat16
F32 = jnp.float32
NN = (((1,), (0,)), ((), ()))
NT = (((1,), (1,)), ((), ()))
TN = (((0,), (0,)), ((), ()))


def mm(a, b, dims):
    return lax.dot_general(a, b, dims, preferred_element_type=F32)


def attend(k, length, q_ref, do_ref, kv_ref, acck, accv, dqs):
    heads = q_ref.shape[1] // HD
    wide = heads * QUARTER
    r0 = k * QUARTER
    keys = NSEL * QB + r0 + QUARTER
    rows = pl.ds(r0, QUARTER)
    seen = pl.ds(0, keys)
    live = (lax.broadcasted_iota(jnp.int32, (QUARTER, 1), 0) + r0) < length
    slices = [pl.ds(h * HD, HD) for h in range(heads)]
    q = jnp.concatenate([q_ref[rows, hs] for hs in slices], axis=0)
    do = jnp.concatenate([jnp.where(live, do_ref[rows, hs], jnp.zeros((), BF)) for hs in slices], axis=0)
    cuts = [(c, c + QUARTER) for c in range(0, keys, QUARTER)]
    s = mm(kv_ref[seen, :HD], q, NT)
    scores = [s[low:high] for low, high in cuts]
    d = mm(kv_ref[seen, HD:], do, NT)
    wgrads = [d[low:high] for low, high in cuts]
    key_pos = lax.broadcasted_iota(jnp.int32, (QUARTER, wide), 0)
    query_pos = lax.broadcasted_iota(jnp.int32, (QUARTER, wide), 1) % QUARTER
    scores[-1] = jnp.where(key_pos <= query_pos, scores[-1], -jnp.inf)
    top = functools.reduce(jnp.maximum, [jnp.max(item, axis=0, keepdims=True) for item in scores])
    exps = [jnp.exp2((item - top) * EXP2_SCALE) for item in scores]
    total = functools.reduce(jnp.add, [jnp.sum(e, axis=0, keepdims=True) for e in exps])
    inverse = 1.0 / total
    delta = inverse * functools.reduce(
        jnp.add, [jnp.sum(e * w, axis=0, keepdims=True) for e, w in zip(exps, wgrads)]
    )
    weights = [e * inverse for e in exps]
    low = jnp.concatenate([p.astype(BF) for p in weights], axis=0)
    ds = jnp.concatenate([(p * (w - delta)).astype(BF) for p, w in zip(weights, wgrads)], axis=0)
    dv = mm(low, do, NN)
    dk = mm(ds, q, NN)
    if k % 2 == 0:
        rest = pl.ds(keys, QUARTER)
        accv[seen, :] = dv
        acck[seen, :] = dk
        accv[rest, :] = jnp.zeros((QUARTER, HD), F32)
        acck[rest, :] = jnp.zeros((QUARTER, HD), F32)
    else:
        accv[seen, :] += dv
        acck[seen, :] += dk
    dq = (mm(kv_ref[seen, :HD].T, ds, NN) * SCALE).T.astype(BF)
    for h, hs in enumerate(slices):
        dqs[pl.ds((k % 2) * QUARTER, QUARTER), hs] = dq[h * QUARTER:(h + 1) * QUARTER]


def kernel(
    q_hbm, do_hbm, rkv, pkv, w_hbm, blocks, lengths,
    x_hbm, pg_hbm, rg_hbm,
    x_out, pg_out, rg_out, out_sem,
    qv, dov, wv, kvg, kvs, acck, accv, dqs,
    part_x, part_y, relay_buf, x1_buf, y1_buf, x2_buf, y2_buf, pp, p0_buf, p1_buf, p2_buf,
    load_sem, ag_s, ag_r, cg_s, cg_r, relay_s, relay_r,
    x1_s, x1_r, y1_s, y1_r, x2_s, x2_r, y2_s, y2_r, p0_s, p0_r, p1_s, p1_r, p2_s, p2_r,
):
    r = lax.axis_index("resp")
    t = lax.axis_index("tp")
    core = r % 2
    chip = r // 2
    y_lo = chip // 4
    z = chip % 4
    x = t // 2
    yh = t % 2
    other = 1 - yh
    after = (x + 1) % 4
    before = (x + 3) % 4
    across = (x + 2) % 4

    def remote(src, dst, ss, rs, device):
        return pltpu.make_async_remote_copy(
            src_ref=src, dst_ref=dst, send_sem=ss, recv_sem=rs,
            device_id=device, device_id_type=MESH,
        )

    sibling = (chip * 2 + 1 - core, t)
    y_mate = (r, x * 2 + other)

    def x_mate(xp):
        return (r, xp * 2 + yh)

    def chip_at(dy, dz):
        return ((y_lo + dy) % 2) * 4 + (z + dz) % 4

    def chip_mate(cp):
        return (cp * 2 + core, t)

    steps = [(0, 1), (0, 3), (1, 0), (0, 2), (1, 1), (1, 3), (1, 2)]

    loads = [
        pltpu.make_async_copy(q_hbm, qv, load_sem.at[0]),
        pltpu.make_async_copy(do_hbm, dov, load_sem.at[1]),
    ]
    w_loads = [pltpu.make_async_copy(w_hbm, wv, load_sem.at[2])]
    for copy in loads + w_loads:
        copy.start()

    barrier = pltpu.get_barrier_semaphore()
    mates = [sibling, y_mate, x_mate(after), x_mate(across), x_mate(before)]
    mates += [chip_mate(chip_at(dy, dz)) for dy, dz in steps]
    for mate in mates:
        pl.semaphore_signal(barrier, inc=1, device_id=mate, device_id_type=MESH)
    pl.semaphore_wait(barrier, len(mates))

    def prompt_rows(cp, c):
        return kvg.at[pl.ds(pl.multiple_of((cp * 2 + c) * 128, 128), 128), :]

    def ag_copy(to_chip, slot_chip):
        return remote(pkv, prompt_rows(slot_chip, core), ag_s.at[to_chip], ag_r.at[slot_chip], chip_mate(to_chip))

    def cg_copy(cp, c):
        return remote(prompt_rows(cp, c), prompt_rows(cp, c), cg_s.at[cp], cg_r.at[cp], sibling)

    for dy, dz in steps:
        ag_copy(chip_at(dy, dz), chip).start()
    kvg[pl.ds(pl.multiple_of(r * 128, 128), 128), :] = pkv[...]
    cg_copy(chip, core).start()
    for copy in loads:
        copy.wait()
    for dy, dz in steps:
        src = chip_at(dy, dz)
        ag_copy(src, src).wait_recv()
        cg_copy(src, core).start()
    for dy, dz in [(0, 0)] + steps:
        cg_copy(chip_at(dy, dz), 1 - core).wait_recv()

    def relay_copy(ch, side):
        return remote(
            part_x.at[ch, across, side], relay_buf.at[ch, side], relay_s.at[ch, side], relay_r.at[ch, side],
            x_mate(after if side == 0 else before),
        )

    def x1_copy(ch, side, half):
        to = after if side == 0 else before
        return remote(
            part_x.at[ch, to, half], x1_buf.at[ch, side, half], x1_s.at[ch, side, half], x1_r.at[ch, side, half],
            x_mate(to),
        )

    def y1_copy(ch, i):
        pair = pl.ds(2 * i, 2)
        return remote(part_y.at[ch, other, pair], y1_buf.at[ch, pair], y1_s.at[ch, i], y1_r.at[ch, i], y_mate)

    def x2_copy(ch, xp, slot):
        return remote(part_y.at[ch, yh, xp], x2_buf.at[ch, slot], x2_s.at[ch, xp], x2_r.at[ch, slot], x_mate(xp))

    def y2_copy(ch):
        return remote(part_x.at[ch, x, other], y2_buf.at[ch], y2_s.at[ch], y2_r.at[ch], y_mate)

    def each_chunk(body, first=0, last=NC):
        def run(ch, carry):
            body(ch)
            return carry

        lax.fori_loop(first, last, run, 0)

    def project(i):
        def body(ch):
            cols = wv[pl.ds(pl.multiple_of(ch * (CX + CY), CX + CY), CX + CY), :]
            out = mm(dqs[...], cols, NT).astype(BF)
            for n in range(4):
                part_x[ch, 2 * i + n // 2, n % 2] = out[n * ROWS:(n + 1) * ROWS, :CX]
                part_y[ch, n % 2, 2 * i + n // 2] = out[n * ROWS:(n + 1) * ROWS, CX:]
            y1_copy(ch, i).start()

            @pl.when(across // 2 == i)
            def _():
                relay_copy(ch, 0).start()
                relay_copy(ch, 1).start()

            @pl.when(after // 2 == i)
            def _():
                x1_copy(ch, 0, 1).start()

            @pl.when(before // 2 == i)
            def _():
                x1_copy(ch, 1, 0).start()

        each_chunk(body)

    def pass_on(i):
        def body(ch):
            for side, to in ((0, after), (1, before)):
                @pl.when(to // 2 == i)
                def _():
                    relay_copy(ch, side).wait_recv()
                    mine = part_x[ch, to, side].astype(F32)
                    part_x[ch, to, side] = (mine + relay_buf[ch, side].astype(F32)).astype(BF)
                    x1_copy(ch, side, side).start()

        each_chunk(body)

    def second_y(i, first, last):
        def body(ch):
            y1_copy(ch, i).wait_recv()
            for n in range(2):
                k = 2 * i + n
                part_y[ch, yh, k] = (part_y[ch, yh, k].astype(F32) + y1_buf[ch, k].astype(F32)).astype(BF)

                @pl.when(k != x)
                def _():
                    x2_copy(ch, k, x).start()

        each_chunk(body, first, last)

    def second_x(i):
        def body(ch):
            acc = part_x[ch, x, other].astype(F32)
            for side in range(2):
                x1_copy(ch, side, other).wait_recv()
                acc += x1_buf[ch, side, other].astype(F32)
            part_x[ch, x, other] = acc.astype(BF)
            y2_copy(ch).start()

        @pl.when(x // 2 == i)
        def _():
            each_chunk(body)

    def step(s, carry):
        i = (s + core) % 2
        done = 1 - i

        for b in range(2):
            @pl.when(i == b)
            def _():
                for j in range(NSEL):
                    listed = jnp.full((QB, 2 * HD), blocks[b, j], jnp.int32)
                    chosen = kvg[pl.ds(0, QB), :]
                    for p in range(1, 8):
                        chosen = jnp.where(listed == p, kvg[pl.ds(p * QB, QB), :], chosen)
                    kvs[pl.ds(j * QB, QB), :] = chosen
                own = (b + 1) * QB
                kvs[pl.ds(NSEL * QB, own), :] = rkv[pl.ds(0, own), :]

        for n in range(2):
            for b in range(2):
                @pl.when(i == b)
                def _():
                    attend(2 * b + n, lengths[0], qv, dov, kvs, acck.at[b], accv.at[b], dqs)

            @pl.when(s == 1)
            def _():
                if n == 0:
                    pass_on(done)
                else:
                    second_y(done, 0, EARLY)
                    second_x(done)

        @pl.when(s == 0)
        def _():
            for copy in w_loads:
                copy.wait()

        project(i)
        return carry

    lax.fori_loop(0, 2, step, 0)
    first_half = core
    last_half = 1 - core
    second_y(first_half, EARLY, NC)

    def prompt_sum(b, carry):
        sum_k = jnp.zeros((QB, HD), F32)
        sum_v = jnp.zeros((QB, HD), F32)
        for i in range(2):
            for j in range(NSEL):
                hit = jnp.full((QB, HD), blocks[i, j], jnp.int32) == b
                sum_k += jnp.where(hit, acck[i, pl.ds(j * QB, QB), :], 0.0)
                sum_v += jnp.where(hit, accv[i, pl.ds(j * QB, QB), :], 0.0)
        both = jnp.concatenate([sum_k * SCALE, sum_v], axis=1).astype(BF)
        pp[0, b % 4, b // 4] = both[:128]
        pp[1, b % 4, b // 4] = both[128:]
        return carry

    lax.fori_loop(0, 8, prompt_sum, 0)
    p0_copy = remote(pp.at[1 - core], p0_buf, p0_s.at[0], p0_r.at[0], sibling)
    p0_copy.start()

    def p1_copy(zp, slot):
        return remote(pp.at[core, zp], p1_buf.at[slot], p1_s.at[zp], p1_r.at[slot], chip_mate(y_lo * 4 + zp))

    p2_copy = remote(pp.at[core, z, 1 - y_lo], p2_buf, p2_s.at[0], p2_r.at[0], chip_mate(chip_at(1, 0)))

    pass_on(last_half)

    p0_copy.wait()

    def p_add(b, carry):
        for half in range(2):
            pp[core, b, half] = (pp[core, b, half].astype(F32) + p0_buf[b, half].astype(F32)).astype(BF)
        return carry

    lax.fori_loop(0, 4, p_add, 0)
    for dz in (2, 1, 3):
        p1_copy((z + dz) % 4, z).start()

    own0 = pl.ds(NSEL * QB, QB)
    own1 = pl.ds((NSEL + 1) * QB, QB)
    rg_out[pl.ds(0, QB), :HD] = (acck[0, own0, :] + acck[1, own0, :]) * SCALE
    rg_out[pl.ds(0, QB), HD:] = accv[0, own0, :] + accv[1, own0, :]
    rg_out[pl.ds(QB, QB), :HD] = acck[1, own1, :] * SCALE
    rg_out[pl.ds(QB, QB), HD:] = accv[1, own1, :]
    rg_copy = pltpu.make_async_copy(rg_out, rg_hbm, out_sem.at[2 * NC])
    rg_copy.start()

    second_y(last_half, 0, 3)
    second_x(last_half)
    second_y(last_half, 3, NC)

    for dz in (1, 3, 2):
        src = (z + dz) % 4
        p1_copy(src, src).wait_recv()
    for_mate = pp[core, z, 1 - y_lo].astype(F32)
    total = pp[core, z, y_lo].astype(F32)
    for dz in (1, 3, 2):
        for_mate += p1_buf[(z + dz) % 4, 1 - y_lo].astype(F32)
        total += p1_buf[(z + dz) % 4, y_lo].astype(F32)
    pp[core, z, 1 - y_lo] = for_mate.astype(BF)
    p2_copy.start()

    def out_copy(ch, kind):
        start, size = ((0, CX), (CX, CY))[kind]
        cols = pl.ds(pl.multiple_of(ch * (CX + CY) + start, 128), size)
        return pltpu.make_async_copy(x_out.at[:, cols], x_hbm.at[:, cols], out_sem.at[2 * ch + kind])

    def last_x(ch):
        acc = part_x[ch, x, yh].astype(F32)
        for side in range(2):
            x1_copy(ch, side, yh).wait_recv()
            acc += x1_buf[ch, side, yh].astype(F32)
        y2_copy(ch).wait_recv()
        acc += y2_buf[ch].astype(F32)
        x_out[:, pl.ds(pl.multiple_of(ch * (CX + CY), 128), CX)] = acc.astype(BF)
        out_copy(ch, 0).start()

    def last_y(ch):
        acc = part_y[ch, yh, x].astype(F32)
        for src in (after, before, across):
            x2_copy(ch, src, src).wait_recv()
            acc += x2_buf[ch, src].astype(F32)
        x_out[:, pl.ds(pl.multiple_of(ch * (CX + CY) + CX, 128), CY)] = acc.astype(BF)
        out_copy(ch, 1).start()

    each_chunk(last_x)
    p2_copy.wait()
    pg_out[...] = total + p2_buf[...].astype(F32)
    pg_copy = pltpu.make_async_copy(pg_out, pg_hbm, out_sem.at[2 * NC + 1])
    pg_copy.start()
    each_chunk(last_y)

    def sent(ch):
        for side in range(2):
            relay_copy(ch, side).wait_send()
            for half in range(2):
                x1_copy(ch, side, half).wait_send()
        y2_copy(ch).wait_send()
        for kind in range(2):
            out_copy(ch, kind).wait()
        for i in range(2):
            y1_copy(ch, i).wait_send()
        for xp in (after, before, across):
            x2_copy(ch, xp, x).wait_send()

    each_chunk(sent)
    rg_copy.wait()
    pg_copy.wait()
    for dy, dz in steps:
        ag_copy(chip_at(dy, dz), chip).wait_send()
    for dz in (1, 2, 3):
        p1_copy((z + dz) % 4, z).wait_send()
    for dy, dz in [(0, 0)] + steps:
        cg_copy(chip_at(dy, dz), core).wait_send()


def hand_over(x_in, pg_in, rg_in, x_to, pg_to, rg_to, x_v, pg_v, rg_v, in_sem, out_sem):
    pieces = []
    for source, held, target, count in ((x_in, x_v, x_to, 4), (rg_in, rg_v, rg_to, 4), (pg_in, pg_v, pg_to, 1)):
        rows = source.shape[0] // count
        pieces += [(source, held, target, pl.ds(n * rows, rows)) for n in range(count)]
    ins = [pltpu.make_async_copy(s.at[c], v.at[c], in_sem.at[n]) for n, (s, v, _, c) in enumerate(pieces)]
    outs = [pltpu.make_async_copy(v.at[c], o.at[c], out_sem.at[n]) for n, (_, v, o, c) in enumerate(pieces)]
    for copy in ins:
        copy.start()
    for copy_in, copy_out in zip(ins, outs):
        copy_in.wait()
        copy_out.start()
    for copy in outs:
        copy.wait()


def on_device(queries, out_grad, resp_kv, prefix_kv, q_weight, block_list, lengths):
    vmem = pl.BlockSpec(memory_space=pltpu.VMEM)
    smem = pl.BlockSpec(memory_space=pltpu.SMEM)
    hbm = pl.BlockSpec(memory_space=pl.ANY)
    dma = pltpu.SemaphoreType.DMA
    results = pl.pallas_call(
        kernel,
        out_shape=(
            jax.ShapeDtypeStruct((ROWS, q_weight.shape[0]), BF),
            jax.ShapeDtypeStruct(prefix_kv.shape, F32),
            jax.ShapeDtypeStruct(resp_kv.shape, F32),
        ),
        in_specs=[hbm, hbm, vmem, vmem, hbm, smem, smem],
        out_specs=(hbm, hbm, hbm),
        scratch_shapes=[
            pltpu.VMEM((ROWS, q_weight.shape[0]), BF),
            pltpu.VMEM(prefix_kv.shape, F32),
            pltpu.VMEM(resp_kv.shape, F32),
            dma((2 + 2 * NC,)),
            pltpu.VMEM(queries.shape, BF),
            pltpu.VMEM(out_grad.shape, BF),
            pltpu.VMEM(q_weight.shape, BF),
            pltpu.VMEM((2048, 256), BF),
            pltpu.VMEM((1280, 256), BF),
            pltpu.VMEM((2, 1280, HD), F32),
            pltpu.VMEM((2, 1280, HD), F32),
            pltpu.VMEM((QB, queries.shape[1]), BF),
            pltpu.VMEM((NC, 4, 2, ROWS, CX), BF),
            pltpu.VMEM((NC, 2, 4, ROWS, CY), BF),
            pltpu.VMEM((NC, 2, ROWS, CX), BF),
            pltpu.VMEM((NC, 2, 2, ROWS, CX), BF),
            pltpu.VMEM((NC, 4, ROWS, CY), BF),
            pltpu.VMEM((NC, 4, ROWS, CY), BF),
            pltpu.VMEM((NC, ROWS, CX), BF),
            pltpu.VMEM((2, 4, 2, 128, 256), BF),
            pltpu.VMEM((4, 2, 128, 256), BF),
            pltpu.VMEM((4, 2, 128, 256), BF),
            pltpu.VMEM((128, 256), BF),
            dma((3,)),
            dma((8,)), dma((8,)), dma((8,)), dma((8,)),
            dma((NC, 2)), dma((NC, 2)),
            dma((NC, 2, 2)), dma((NC, 2, 2)),
            dma((NC, 2)), dma((NC, 2)),
            dma((NC, 4)), dma((NC, 4)),
            dma((NC,)), dma((NC,)),
            dma((1,)), dma((1,)),
            dma((4,)), dma((4,)),
            dma((1,)), dma((1,)),
        ],
        compiler_params=pltpu.CompilerParams(
            collective_id=0, has_side_effects=True, vmem_limit_bytes=56 * 1024 * 1024
        ),
        cost_estimate=pl.CostEstimate(flops=12_000_000_000, bytes_accessed=16_000_000, transcendentals=5_000_000),
        name="attention_backward",
    )(queries, out_grad, resp_kv, prefix_kv, q_weight, block_list, lengths)
    return pl.pallas_call(
        hand_over,
        out_shape=tuple(jax.ShapeDtypeStruct(item.shape, item.dtype) for item in results),
        in_specs=[hbm] * 3,
        out_specs=(hbm, hbm, hbm),
        scratch_shapes=[pltpu.VMEM(item.shape, item.dtype) for item in results] + [dma((9,)), dma((9,))],
        name="hand_over",
    )(*results)


def solution(mesh):
    return jax.shard_map(
        on_device,
        mesh=mesh,
        in_specs=(
            P("resp", "tp"),
            P("resp", "tp"),
            P("resp", "tp"),
            P("resp", "tp"),
            P(None, "tp"),
            P("resp", None),
            P("resp"),
        ),
        out_specs=(P(("resp", "tp"), None), P("resp", "tp"), P("resp", "tp")),
        check_vma=False,
    )
```
